32 devices in a mesh: src: 4 (over y, x), dst: 8 (over z, core).
Axes of the slice: x: 2, y: 2, z: 4, core: 2. Of those that a mesh axis runs over, the one named last changes fastest.
Arguments:
- density0: float32 [16, 16384], P(None, ('src', 'dst')), may hold values from 0.2 to 5
- logits: float32 [2, 16, 16384], P(None, None, ('src', 'dst')), may hold values from -6 to 6
- value_final: float32 [16, 16384], P(None, ('src', 'dst')), may hold values from -6 to 6
- base_reward: float32 [2, 16, 16384], P(None, None, ('src', 'dst')), may hold values from -6 to 6
- crowd: float32 [16], replicated, may hold values from 0.2 to 2
- tiles: bfloat16 [4, 8, 2, 8, 256, 256], P('src', 'dst'), may hold values from 0 to 0.75
- tile_src: int32 [4, 8, 2, 8], P('src', 'dst'), may hold values from 0 to 15
- tile_dst: int32 [4, 8, 2, 8], P('src', 'dst'), may hold values from 0 to 7
- tile_count: int32 [4, 8, 2], P('src', 'dst'), may hold values from 2 to 8, as said below
Outputs:
- new_logits: float32 [2, 16, 16384], P(None, None, ('src', 'dst'))
- value_start: float32 [16, 16384], P(None, ('src', 'dst'))
- density_final: float32 [16, 16384], P(None, ('src', 'dst'))
The draws below stay inside these ranges and needn't reach their ends.
Inputs may be any that keep to these rules, and one draw needn't show every extreme that they name: `tile_count`: slots at or past the count are ignored. In every draw some device holds 8 live slots for some action.
All inputs are finite; a program needn't handle non-finite values.
Results may differ from the reference program's by a relative error of at most 0.0011.
Values may be sent and summed in bfloat16 or wider, within the bound.
A program may use at most 64 MiB of HBM per device.

```python
import math
import jax
import jax.numpy as jnp
from jax import lax

P_SIZE = 16
A = 2
B = 256
BPZ = 2
TCAP = 8
H = 4
BS_SRC = 16
BS_DST = 8
NSTATES = 16384
N_SRC = 4
N_DST = 8


def draw_tile_count(key, part):
    first, second, third = jax.random.split(jax.random.fold_in(key, 17), 3)
    shape = (N_SRC, N_DST, A)
    base = jax.random.randint(first, shape, TCAP // 4, TCAP // 2 + 1)
    hubs = jax.random.randint(second, shape, 0, 8) == 0
    forced = jax.random.randint(third, (), 0, N_SRC * N_DST * A)
    flat_index = jnp.arange(N_SRC * N_DST * A, dtype=jnp.int32).reshape(shape)
    chosen = jnp.logical_or(hubs, flat_index == forced)
    return jnp.where(chosen, TCAP, base).astype(jnp.int32)


def draw_tiles(key, part):
    keys = jax.random.split(jax.random.fold_in(key, 29), 4)
    lead = (N_SRC, N_DST, A, TCAP)
    offset = jax.random.randint(keys[0], lead + (1, 1), 0, B)
    jitter = jax.random.randint(keys[1], lead + (B, 1), -2, 3)
    band = jax.random.randint(keys[2], lead + (B, 1), 8, 17)
    rows = jnp.arange(B, dtype=jnp.int32)[:, None]
    cols = jnp.arange(B, dtype=jnp.int32)[None, :]
    first_col = rows + offset + jitter - band // 2
    inside = jnp.mod(cols - first_col, B) < band
    factor_scale = 2.0 * BPZ / (TCAP * 37.0)
    factor = jnp.exp(1.5 * jax.random.truncated_normal(keys[3], -2.5, 2.5, lead + (B, B), jnp.float32))
    values = factor * factor_scale
    return jnp.where(inside, values, 0.0).astype(jnp.bfloat16)


def touch_ends(values, stream_key, smallest, top_value):
    shape = values.shape
    index_at = [jax.random.randint(jax.random.fold_in(stream_key, axis), (), 0, shape[axis]) for axis in range(len(shape))]
    values = values.at[tuple(index_at)].set(smallest)
    longest = shape.index(max(shape))
    index_at[longest] = (index_at[longest] + 1) % shape[longest]
    return values.at[tuple(index_at)].set(top_value)


def steps_of(own_key, dims, pieces, low, high):
    factor_of, own = 1.0, jax.random.fold_in(own_key, 6)
    for dim, blocks in pieces:
        heights = jnp.exp(jax.random.uniform(jax.random.fold_in(own, dim), (blocks,), jnp.float32, low / len(pieces), high / len(pieces)))
        factor_of = factor_of * jnp.repeat(heights, dims[dim] // blocks).reshape([-1 if axis == dim else 1 for axis in range(len(dims))])
    return factor_of


def normal_values(rng, dims, scale, bound, cuts=(), kind=jnp.bfloat16):
    values = jax.random.normal(rng, dims, jnp.float32) * scale
    if len(cuts) > 0:
        values = steps_of(rng, dims, cuts, -0.22, 0.18) * values
    return jnp.clip(values, min=-bound, max=bound).astype(kind)


def setup_inputs(seed: int = 0) -> dict:
    streams_of = jax.random.split(jax.random.key(seed), 10)
    density0 = jnp.clip(jnp.exp(math.log(5.0) - 3.218876 * jax.random.uniform(streams_of[0], (P_SIZE, NSTATES), jnp.float32) ** steps_of(streams_of[0], (P_SIZE, NSTATES), ((1, 32),), -0.2, 0.2)), 0.2, 5.0)
    logits = normal_values(streams_of[1], (A, P_SIZE, NSTATES), 1.0, 6.0, ((2, 32),), jnp.float32)
    value_final = normal_values(streams_of[2], (P_SIZE, NSTATES), 1.0, 6.0, ((1, 32),), jnp.float32)
    base_reward = normal_values(streams_of[3], (A, P_SIZE, NSTATES), 1.0, 6.0, ((2, 32),), jnp.float32)
    crowd = jnp.clip(jnp.exp(jax.random.uniform(streams_of[4], (P_SIZE,), jnp.float32, math.log(0.2), math.log(2.0))), 0.2, 2.0)
    tiles = draw_tiles(jax.random.fold_in(streams_of[9], 71), 0)
    tile_src = touch_ends(jax.random.randint(streams_of[6], (N_SRC, N_DST, A, TCAP), 0, BS_SRC), jax.random.fold_in(streams_of[6], 1), 0, BS_SRC - 1).astype(jnp.int32)
    tile_dst = touch_ends(jax.random.randint(streams_of[7], (N_SRC, N_DST, A, TCAP), 0, BS_DST), jax.random.fold_in(streams_of[7], 1), 0, BS_DST - 1).astype(jnp.int32)
    tile_count = draw_tile_count(jax.random.fold_in(streams_of[9], 71), 0)
    return dict(density0=density0, logits=logits, value_final=value_final, base_reward=base_reward, crowd=crowd, tiles=tiles, tile_src=tile_src, tile_dst=tile_dst, tile_count=tile_count)


discount = 0.9
step_size = 1.0


def policy_of(logits):
    margin = logits[0] - logits[1]
    return jnp.stack([jax.nn.sigmoid(margin), jax.nn.sigmoid(-margin)])


def reward_of(base_reward, crowd, density):
    crowding = jnp.log1p(jnp.mean(density, axis=0))
    return base_reward - crowd[None, :, None] * crowding[None, None, :]


def take_rows(block_set, row_index):
    return jnp.take(block_set, row_index, axis=1)


def add_rows(target, row_index, update):
    return target.at[:, row_index, :].add(update)


def reference(density0, logits, value_final, base_reward, crowd, tiles, tile_src, tile_dst, tile_count):
    device_total = N_SRC * N_DST
    blocks_all = NSTATES // B
    src_index = jnp.arange(N_SRC, dtype=jnp.int32)[:, None, None, None]
    dst_index = jnp.arange(N_DST, dtype=jnp.int32)[None, :, None, None]
    src_global = (src_index * BS_SRC + tile_src).astype(jnp.int32)
    dst_global = (((tile_dst // BPZ) * N_DST + dst_index) * BPZ + tile_dst % BPZ).astype(jnp.int32)
    slot_index = jnp.arange(TCAP, dtype=jnp.int32)[None, None, None, :]
    live = (slot_index < tile_count[..., None]).astype(jnp.float32)
    tile_flat = tiles.reshape(device_total, A, TCAP, B, B)
    src_flat = src_global.reshape(device_total, A, TCAP)
    dst_flat = dst_global.reshape(device_total, A, TCAP)
    live_flat = live.reshape(device_total, A, TCAP)
    policy_now = policy_of(logits)

    def forward_raw(weighted):
        blocks = weighted.reshape(A, P_SIZE, blocks_all, B)

        def visit(accum, item):
            tile_block, src_rows, dst_rows, active = item
            picked = jax.vmap(take_rows)(blocks, src_rows)
            product = jnp.einsum('apki,akij->apkj', picked.astype(jnp.float32), tile_block.astype(jnp.float32), precision=lax.Precision.HIGHEST)
            product = product * active[:, None, :, None]
            flat = jnp.transpose(product, (1, 0, 2, 3)).reshape(P_SIZE, A * TCAP, B)
            return accum.at[:, dst_rows.reshape(-1), :].add(flat), None

        start = jnp.zeros((P_SIZE, blocks_all, B), jnp.float32)
        result, _ = lax.scan(visit, start, (tile_flat, src_flat, dst_flat, live_flat))
        return result.reshape(P_SIZE, NSTATES)

    def backward_raw(value_half):
        blocks = value_half.reshape(P_SIZE, blocks_all, B)

        def pick_columns(dst_action):
            return jnp.take(blocks, dst_action, axis=1)

        def visit(accum, item):
            tile_block, src_rows, dst_rows, active = item
            picked = jax.vmap(pick_columns)(dst_rows)
            product = jnp.einsum('akij,apkj->apki', tile_block.astype(jnp.float32), picked.astype(jnp.float32), precision=lax.Precision.HIGHEST)
            product = product * active[:, None, :, None]
            return jax.vmap(add_rows)(accum, src_rows, product), None

        start = jnp.zeros((A, P_SIZE, blocks_all, B), jnp.float32)
        result, _ = lax.scan(visit, start, (tile_flat, src_flat, dst_flat, live_flat))
        return result.reshape(A, P_SIZE, NSTATES)

    densities = [density0]
    for moment in range(H):
        weighted = (policy_now * densities[-1][None]).astype(jnp.bfloat16)
        arrived = forward_raw(weighted)
        mass = jnp.sum(arrived, axis=1)
        densities.append(arrived * (NSTATES / mass)[:, None])

    value_next = value_final
    action_value = base_reward
    for moment in reversed(range(H)):
        returned = backward_raw(value_next.astype(jnp.bfloat16))
        action_value = reward_of(base_reward, crowd, densities[moment]) + discount * returned
        value_next = jnp.sum(policy_now * action_value, axis=0)
    new_logits = logits + step_size * action_value
    return (new_logits, value_next, densities[-1])
```

```python
import functools

import jax
import jax.numpy as jnp
from jax import lax
from jax.experimental import pallas as pl
from jax.experimental.pallas import tpu as pltpu
from jax.sharding import PartitionSpec as P

H = 4
LANES = 128
DISCOUNT = 0.9
STEP_SIZE = 1.0
MESH = pl.DeviceIdType.MESH
F32 = jnp.float32
BF16 = jnp.bfloat16


def kernel(
    S, D, N, B, BPZ, A, K,
    density0, logits, value_final, base_reward, crowd, tiles_hbm, tile_src, tile_dst, tile_count,
    new_logits, value_start, density_final,
    tiles, wbuf, pol, margin, lhs, mask, prod,
    rs_send, rs_recv, ag_send, ag_recv, ag3_send, ag3_recv, ms_send, ms_recv,
    vb0, vb1, vb2, vb3, w0buf, vr_send, vr_recv, vz_send, vz_recv, own,
    tile_sem, rs_ss, rs_rs, ag_ss, ag_rs, w0_ss, w0_rs, mg_ss, mg_rs, ms_ss, ms_rs,
    va_ss, va_rs, vr_ss, vr_rs,
):
    vbuf = (vb0, vb1, vb2, vb3)
    s = lax.axis_index("src")
    d = lax.axis_index("dst")
    PN = density0.shape[0]
    W = BPZ * B
    SB, DB = BPZ * D, BPZ * S
    src_peers = [lax.rem(s + r, S) for r in range(S)]
    dst_peers = [lax.rem(d + r, D) for r in range(D)]
    src_back = [lax.rem(s + S - r, S) for r in range(S)]
    dst_back = [lax.rem(d + D - r, D) for r in range(D)]

    def to_src(src, dst, ss, rs, r):
        return pltpu.make_async_remote_copy(
            src_ref=src, dst_ref=dst, send_sem=ss, recv_sem=rs,
            device_id=(src_peers[r], d), device_id_type=MESH)

    def to_dst(src, dst, ss, rs, r):
        return pltpu.make_async_remote_copy(
            src_ref=src, dst_ref=dst, send_sem=ss, recv_sem=rs,
            device_id=(s, dst_peers[r]), device_id_type=MESH)

    tile_copy = pltpu.make_async_copy(tiles_hbm, tiles, tile_sem)
    tile_copy.start()
    barrier = pltpu.get_barrier_semaphore()
    for r in range(1, S):
        pl.semaphore_signal(barrier, inc=1, device_id=(src_peers[r], d), device_id_type=MESH)
    for r in range(1, D):
        pl.semaphore_signal(barrier, inc=1, device_id=(s, dst_peers[r]), device_id_type=MESH)

    gap = logits[0] - logits[1]
    p0, p1 = jax.nn.sigmoid(gap), jax.nn.sigmoid(-gap)
    rho = density0[...]
    vf = value_final[...].astype(BF16)
    for b in range(BPZ):
        cols = slice(b * B, (b + 1) * B)
        w0buf[0, BPZ * d + b] = (p0 * rho)[:, cols].astype(BF16)
        w0buf[1, BPZ * d + b] = (p1 * rho)[:, cols].astype(BF16)
        margin[BPZ * d + b] = gap[:, cols]
        vbuf[3][BPZ * s + b] = vf[:, cols]
    pl.semaphore_wait(barrier, S + D - 2)

    pending = []

    def start(copy):
        copy.start()
        pending.append(copy)
        return copy

    mine = pl.ds(BPZ * d, BPZ)
    w0 = [start(to_dst(w0buf.at[:, mine], w0buf.at[:, mine], w0_ss.at[r - 1], w0_rs.at[r - 1], r)) for r in range(1, D)]

    def send_value(t):
        at = vbuf[t].at[pl.ds(BPZ * s, BPZ)]
        return [start(to_src(at, at, va_ss.at[t, r - 1], va_rs.at[t, r - 1], r)) for r in range(1, S)]

    va = {3: send_value(3)}
    mg = [start(to_dst(margin.at[mine], margin.at[mine], mg_ss.at[r - 1], mg_rs.at[r - 1], r)) for r in range(1, D)]

    for a in range(A):
        for k in range(K):
            live = jnp.where(k < tile_count[0, 0, a], 1.0, 0.0).astype(F32)
            for c in range(DB):
                hit = jnp.where(tile_dst[0, 0, a, k] == c, live, 0.0)
                mask[(a * K + k) * DB + c] = jnp.full((PN, LANES), hit, F32).astype(BF16)
    row = lax.broadcasted_iota(jnp.int32, (PN, W), 0)
    crowd_col = jnp.zeros((PN, W), F32)
    for p in range(PN):
        crowd_col = jnp.where(row == p, crowd[p], crowd_col)
    own[4] = crowd_col
    own[5] = p0
    own[6] = p1
    lane = lax.broadcasted_iota(jnp.int32, (PN, LANES), 1)

    def push(t):
        for a in range(A):
            for k in range(K):
                w = (w0buf if t == 0 else wbuf)[a, tile_src[0, 0, a, k]]
                q = a * K + k
                for c in range(DB):
                    m = mask[q * DB + c]
                    lhs[c * PN:(c + 1) * PN, q * B:(q + 1) * B] = w * jnp.concatenate([m] * (B // LANES), axis=1)
        arrived = jnp.dot(lhs[...], tiles[...], preferred_element_type=F32)
        total = arrived[0:PN]
        for c in range(1, DB):
            total = total + arrived[c * PN:(c + 1) * PN]
        lanes = sum(total[:, i:i + LANES] for i in range(0, B, LANES))
        for c in range(DB):
            rs_send[t, c // BPZ, :, (c % BPZ) * B:(c % BPZ + 1) * B] = arrived[c * PN:(c + 1) * PN]
        for c in range(S):
            rs_send[t, c, :, W:W + LANES] = lanes
        return [start(to_src(rs_send.at[t, src_peers[r]], rs_recv.at[t, r - 1], rs_ss.at[t, r - 1], rs_rs.at[t, r - 1], r))
                for r in range(1, S)]

    def owned(t, copies):
        total = rs_send[t, s]
        for r in range(1, S):
            copies[r - 1].wait_recv()
            total = total + rs_recv[t, r - 1]
        mass = jnp.sum(total[:, W:W + LANES], axis=1, keepdims=True)
        mass = jnp.broadcast_to(mass, (PN, LANES))
        hi = mass.astype(BF16).astype(F32)
        mid = (mass - hi).astype(BF16).astype(F32)
        low = mass - hi - mid
        packed = jnp.where(lane == 0, hi, jnp.where(lane == 1, mid, jnp.where(lane == 2, low, 0.0)))
        return total[:, :W], packed

    def scale_of(packed):
        mass = jnp.sum(packed, axis=1, keepdims=True)
        return N / mass

    def weigh(block, raw, scale):
        now = raw * scale
        wbuf[0, block] = (pol[0, block] * now).astype(BF16)
        wbuf[1, block] = (pol[1, block] * now).astype(BF16)

    def send_density(t, raw, packed):
        ag_send[t, :, :W] = raw.astype(BF16)
        ag_send[t, :, W:W + LANES] = packed.astype(BF16)
        return [start(to_dst(ag_send.at[t], ag_recv.at[t, r - 1], ag_ss.at[t, r - 1], ag_rs.at[t, r - 1], r))
                for r in range(1, D)]

    def take_density(t, raw, packed, copies):
        for r in range(1, D):
            copies[r - 1].wait_recv()
            packed = packed + ag_recv[t, r - 1, :, W:W + LANES].astype(F32)
        scale = scale_of(packed)
        for b in range(BPZ):
            weigh(BPZ * d + b, raw[:, b * B:(b + 1) * B], scale)
        for r in range(1, D):
            for b in range(BPZ):
                weigh(BPZ * dst_back[r] + b, ag_recv[t, r - 1, :, b * B:(b + 1) * B].astype(F32), scale)
        return raw * scale

    def send_mass(i, packed):
        ms_send[i] = packed.astype(BF16)
        return [start(to_dst(ms_send.at[i], ms_recv.at[i, r - 1], ms_ss.at[i, r - 1], ms_rs.at[i, r - 1], r))
                for r in range(1, D)]

    def take_mass(i, packed, copies):
        for r in range(1, D):
            copies[r - 1].wait_recv()
            packed = packed + ms_recv[i, r - 1].astype(F32)
        return scale_of(packed)

    def pull(t):
        for a in range(A):
            for k in range(K):
                q = a * K + k
                v = vbuf[t][tile_dst[0, 0, a, k]]
                live = jnp.where(k < tile_count[0, 0, a], 1.0, 0.0).astype(F32)
                prod[q] = live * lax.dot_general(
                    v, tiles[q * B:(q + 1) * B, :], (((1,), (1,)), ((), ())), preferred_element_type=F32)

    def collect(a, block):
        out = None
        for k in range(K):
            term = jnp.where(tile_src[0, 0, a, k] == block, 1.0, 0.0).astype(F32) * prod[a * K + k]
            out = term if out is None else out + term
        return out

    def wait_value(t):
        for copy in va[t]:
            copy.wait_recv()

    def spread(t):
        pull(t)

        def step(g, _):
            for b in range(BPZ):
                c = g * BPZ + b
                vr_send[t - 1, c] = (pol[0, c] * collect(0, c) + pol[1, c] * collect(1, c)).astype(BF16)
            return _

        lax.fori_loop(0, D, step, 0)
        return [start(to_dst(vr_send.at[t - 1, pl.ds(BPZ * dst_peers[r], BPZ)], vr_recv.at[t - 1, r - 1],
                             vr_ss.at[t, r - 1], vr_rs.at[t, r - 1], r)) for r in range(1, D)]

    def crowding(t, now):
        own[t] = own[4] * jnp.log(1.0 + jnp.mean(now, axis=0, keepdims=True))

    def gather_value(t, copies):
        for copy in copies:
            copy.wait_recv()
        for b in range(BPZ):
            cols = slice(b * B, (b + 1) * B)
            total = vr_send[t - 1, BPZ * d + b].astype(F32)
            for r in range(1, D):
                total = total + vr_recv[t - 1, r - 1, b].astype(F32)
            q0, q1 = own[5, :, cols], own[6, :, cols]
            reward = q0 * base_reward[0, :, cols] + q1 * base_reward[1, :, cols] - (q0 + q1) * own[t, :, cols]
            vbuf[t - 1][BPZ * s + b] = (reward + DISCOUNT * total).astype(BF16)
        va[t - 1] = send_value(t - 1)

    tile_copy.wait()
    for copy in w0:
        copy.wait_recv()
    rs = push(0)
    crowding(0, rho)
    for copy in mg:
        copy.wait_recv()

    def policy(c, _):
        pol[0, c] = jax.nn.sigmoid(margin[c])
        pol[1, c] = jax.nn.sigmoid(-margin[c])
        return _

    lax.fori_loop(0, SB, policy, 0)
    raw, packed = owned(0, rs)
    ag = send_density(0, raw, packed)
    now = take_density(0, raw, packed, ag)
    rs = push(1)
    crowding(1, now)
    wait_value(3)
    vr = spread(3)
    raw, packed = owned(1, rs)
    ag = send_density(1, raw, packed)
    now = take_density(1, raw, packed, ag)
    rs = push(2)
    crowding(2, now)
    raw, packed = owned(2, rs)
    ms = send_mass(0, packed)
    ag3_send[...] = raw
    scale3 = take_mass(0, packed, ms)
    now = raw * scale3
    crowding(3, now)
    gather_value(3, vr)
    ag = [start(to_dst(ag3_send, ag3_recv.at[r - 1], ag_ss.at[2, r - 1], ag_rs.at[2, r - 1], r)) for r in range(1, D)]
    wait_value(2)
    vr = spread(2)
    for copy in ag:
        copy.wait_recv()
    for b in range(BPZ):
        weigh(BPZ * d + b, raw[:, b * B:(b + 1) * B], scale3)
        for r in range(1, D):
            weigh(BPZ * dst_back[r] + b, ag3_recv[r - 1, :, b * B:(b + 1) * B], scale3)
    gather_value(2, vr)
    rs = push(3)
    wait_value(1)
    vr = spread(1)
    raw, packed = owned(3, rs)
    ms = send_mass(1, packed)
    gather_value(1, vr)
    density_final[...] = raw * take_mass(1, packed, ms)
    wait_value(0)
    pull(0)

    def both(g, _):
        for b in range(BPZ):
            c = g * BPZ + b
            for a in range(A):
                vz_send[a, c] = collect(a, c)
        return _

    lax.fori_loop(0, D, both, 0)
    vr = [start(to_dst(vz_send.at[:, pl.ds(BPZ * dst_peers[r], BPZ)], vz_recv.at[r - 1],
                       vr_ss.at[0, r - 1], vr_rs.at[0, r - 1], r)) for r in range(1, D)]
    for copy in vr:
        copy.wait_recv()
    for b in range(BPZ):
        cols = slice(b * B, (b + 1) * B)
        value = None
        for a in range(A):
            total = vz_send[a, BPZ * d + b]
            for r in range(1, D):
                total = total + vz_recv[r - 1, a, b]
            action_value = base_reward[a, :, cols] - own[0, :, cols] + DISCOUNT * total
            new_logits[a, :, cols] = logits[a, :, cols] + STEP_SIZE * action_value
            term = own[5 + a, :, cols] * action_value
            value = term if value is None else value + term
        value_start[:, cols] = value
    for copy in pending:
        copy.wait_send()


def body(density0, logits, value_final, base_reward, crowd, tiles, tile_src, tile_dst, tile_count):
    S, D = lax.axis_size("src"), lax.axis_size("dst")
    PN, W = density0.shape
    A, K, B = tiles.shape[2], tiles.shape[3], tiles.shape[-1]
    BPZ = W // B
    SB, DB = BPZ * D, BPZ * S
    N = float(W * S * D)
    vmem, smem = pl.BlockSpec(memory_space=pltpu.VMEM), pl.BlockSpec(memory_space=pltpu.SMEM)
    dma = pltpu.SemaphoreType.DMA
    V = pltpu.VMEM
    scratch = [
        V((A * K * B, B), BF16), V((A, SB, PN, B), BF16), V((A, SB, PN, B), F32), V((SB, PN, B), F32),
        V((DB * PN, A * K * B), BF16), V((A * K * DB, PN, LANES), BF16), V((A * K, PN, B), F32),
        V((H, S, PN, W + LANES), F32), V((H, S - 1, PN, W + LANES), F32),
        V((2, PN, W + LANES), BF16), V((2, D - 1, PN, W + LANES), BF16),
        V((PN, W), F32), V((D - 1, PN, W), F32), V((2, PN, LANES), BF16), V((2, D - 1, PN, LANES), BF16),
        *[V((DB, PN, B), BF16)] * H, V((A, SB, PN, B), BF16), V((3, SB, PN, B), BF16), V((3, D - 1, BPZ, PN, B), BF16),
        V((A, SB, PN, B), F32), V((D - 1, A, BPZ, PN, B), F32), V((7, PN, W), F32),
        dma,
        dma((H, S - 1)), dma((H, S - 1)), dma((3, D - 1)), dma((3, D - 1)),
        dma((D - 1,)), dma((D - 1,)), dma((D - 1,)), dma((D - 1,)),
        dma((2, D - 1)), dma((2, D - 1)),
        dma((H, S - 1)), dma((H, S - 1)), dma((H, D - 1)), dma((H, D - 1)),
    ]
    flops = 2 * H * 2 * A * K * PN * B * B
    return pl.pallas_call(
        functools.partial(kernel, S, D, N, B, BPZ, A, K),
        out_shape=(
            jax.ShapeDtypeStruct(logits.shape, F32),
            jax.ShapeDtypeStruct((PN, W), F32),
            jax.ShapeDtypeStruct((PN, W), F32),
        ),
        in_specs=[vmem, vmem, vmem, vmem, smem, pl.BlockSpec(memory_space=pl.ANY), smem, smem, smem],
        out_specs=(vmem, vmem, vmem),
        scratch_shapes=scratch,
        cost_estimate=pl.CostEstimate(flops=flops, bytes_accessed=tiles.size * 2, transcendentals=0),
        compiler_params=pltpu.CompilerParams(
            collective_id=0, has_side_effects=True, vmem_limit_bytes=48 * 1024 * 1024),
    )(density0, logits, value_final, base_reward, crowd, tiles.reshape(A * K * B, B), tile_src, tile_dst, tile_count)


def solution(mesh):
    in_specs = (
        P(None, ("src", "dst")),
        P(None, None, ("src", "dst")),
        P(None, ("src", "dst")),
        P(None, None, ("src", "dst")),
        P(),
        P("src", "dst", None, None, None, None),
        P("src", "dst", None, None),
        P("src", "dst", None, None),
        P("src", "dst", None),
    )
    out_specs = (P(None, None, ("src", "dst")), P(None, ("src", "dst")), P(None, ("src", "dst")))
    return jax.shard_map(body, mesh=mesh, in_specs=in_specs, out_specs=out_specs, check_vma=False)
```

```python
import functools

import jax
import jax.numpy as jnp
from jax import lax
from jax.experimental import pallas as pl
from jax.experimental.pallas import tpu as pltpu
from jax.sharding import PartitionSpec as P

H = 4
LANES = 128
DISCOUNT = 0.9
STEP_SIZE = 1.0
MESH = pl.DeviceIdType.MESH
F32 = jnp.float32
BF16 = jnp.bfloat16


def kernel(
    S, D, N, B, BPZ, A, K,
    density0_h, logits_h, value_final_h, base_reward_h, crowd_h, tiles_h, tile_src_h, tile_dst_h, tile_count_h,
    result,
    density0, logits, value_final, base_reward, crowd, tiles, tile_src, tile_dst, tile_count, in_sem,
    wbuf, w0buf, pol, margin, lhs, mask, prod, arr,
    rs_send, rs_recv, rz_send, rz_recv, ag_send, ag_recv, ag3_send, ag3_recv, ms_send, ms_recv,
    vb0, vb1, vb2, vb3, pr_send, pr_recv, zs_send, zs_recv, zl_send, zl_recv, keep, own,
    rs_ss, rs_rs, sh_ss, sh_rs, ms_ss, ms_rs, va_ss, va_rs, pr_ss, pr_rs, zs_ss, zs_rs,
):
    vbuf = (vb0, vb1, vb2, vb3)
    s = lax.axis_index("src")
    d = lax.axis_index("dst")
    Z = D // 2
    z = d // 2
    core = d - 2 * z
    PN, W = density0.shape
    src_peers = [lax.rem(s + r, S) for r in range(S)]
    dst_peers = [lax.rem(d + r, D) for r in range(D)]
    z_peers = [lax.rem(z + r, Z) for r in range(Z)]
    z_back = [lax.rem(z + Z - r, Z) for r in range(Z)]

    def remote(src, dst, ss, rs, device):
        return pltpu.make_async_remote_copy(
            src_ref=src, dst_ref=dst, send_sem=ss, recv_sem=rs, device_id=device, device_id_type=MESH)

    def to_src(src, dst, ss, rs, r):
        return remote(src, dst, ss, rs, (src_peers[r], d))

    def to_dst(src, dst, ss, rs, r):
        return remote(src, dst, ss, rs, (s, dst_peers[r]))

    def to_z(src, dst, ss, rs, r):
        return remote(src, dst, ss, rs, (s, 2 * z_peers[r] + core))

    def to_pair(src, dst, ss, rs):
        return remote(src, dst, ss, rs, (s, 2 * z + 1 - core))

    loads = [pltpu.make_async_copy(h, v, in_sem.at[i]) for i, (h, v) in enumerate((
        (logits_h, logits), (density0_h, density0), (value_final_h, value_final), (tile_src_h, tile_src),
        (tile_dst_h, tile_dst), (tile_count_h, tile_count), (crowd_h, crowd), (base_reward_h, base_reward),
        (tiles_h, tiles)))]
    for load in loads:
        load.start()
    barrier = pltpu.get_barrier_semaphore()
    for r in range(1, S):
        pl.semaphore_signal(barrier, inc=1, device_id=(src_peers[r], d), device_id_type=MESH)
    for r in range(1, D):
        pl.semaphore_signal(barrier, inc=1, device_id=(s, dst_peers[r]), device_id_type=MESH)

    for load in loads[:3]:
        load.wait()
    gap = logits[0] - logits[1]
    p0, p1 = jax.nn.sigmoid(gap), jax.nn.sigmoid(-gap)
    rho = density0[...]
    vf = value_final[...].astype(BF16)
    for b in range(BPZ):
        cols = slice(b * B, (b + 1) * B)
        w0buf[0, BPZ * d + b] = (p0 * rho)[:, cols].astype(BF16)
        w0buf[1, BPZ * d + b] = (p1 * rho)[:, cols].astype(BF16)
        margin[BPZ * d + b] = gap[:, cols]
        vbuf[3][BPZ * s + b] = vf[:, cols]
    pl.semaphore_wait(barrier, S + D - 2)

    pending = []

    def start(copy):
        copy.start()
        pending.append(copy)
        return copy

    def share(i, own_ref, there):
        ss, rs = sh_ss.at[i], sh_rs.at[i]
        hops = [start(to_z(own_ref, there(r), ss.at[r - 1], rs.at[r - 1], r)) for r in range(1, Z)]
        return hops, start(to_pair(own_ref, there(Z), ss.at[Z - 1], rs.at[Z - 1]))

    def relay(i, shared, here, there):
        ss, rs = sh_ss.at[i], sh_rs.at[i]
        hops, pair = shared
        onward = []
        for r in range(1, Z):
            hops[r - 1].wait_recv()
            onward.append(start(to_pair(here(r), there(r), ss.at[Z - 1 + r], rs.at[Z - 1 + r])))
        pair.wait_recv()
        for copy in onward:
            copy.wait_recv()

    def blocks_of(j):
        return pl.ds(BPZ * j, BPZ)

    def came_from(i):
        return 2 * z_back[i % Z] + (core if i < Z else 1 - core)

    def share_value(t):
        at = vbuf[t].at[pl.ds(BPZ * s, BPZ)]
        return [start(to_src(at, at, va_ss.at[t, r - 1], va_rs.at[t, r - 1], r)) for r in range(1, S)]

    w0_mine = w0buf.at[:, blocks_of(d)]
    w0_here = lambda r: w0buf.at[:, blocks_of(2 * z_back[r] + core)]
    w0 = share(0, w0_mine, lambda r: w0_mine)
    va = {3: share_value(3)}

    for load in loads[3:7]:
        load.wait()
    for a in range(A):
        for k in range(K):
            live = jnp.where(k < tile_count[0, 0, a], 1.0, 0.0).astype(F32)
            for c in range(BPZ * S):
                hit = jnp.where(tile_dst[0, 0, a, k] == c, live, 0.0)
                mask[(a * K + k) * BPZ * S + c] = jnp.full((PN, LANES), hit, F32).astype(BF16)
    row = lax.broadcasted_iota(jnp.int32, (PN, W), 0)
    crowd_col = jnp.zeros((PN, W), F32)
    for p in range(PN):
        crowd_col = jnp.where(row == p, crowd[p], crowd_col)
    own[4] = crowd_col
    own[5] = p0
    own[6] = p1
    lane = lax.broadcasted_iota(jnp.int32, (PN, LANES), 1)
    DB = BPZ * S

    def push(t):
        for a in range(A):
            for k in range(K):
                w = (w0buf if t == 0 else wbuf)[a, tile_src[0, 0, a, k]]
                q = a * K + k
                for c in range(DB):
                    m = mask[q * DB + c]
                    lhs[c * PN:(c + 1) * PN, q * B:(q + 1) * B] = w * jnp.concatenate([m] * (B // LANES), axis=1)
        arrived = jnp.dot(lhs[...], tiles[...], preferred_element_type=F32)
        total = arrived[0:PN]
        for c in range(1, DB):
            total = total + arrived[c * PN:(c + 1) * PN]
        mass = jnp.broadcast_to(jnp.sum(total, axis=1, keepdims=True), (PN, LANES))
        hi = mass.astype(BF16).astype(F32)
        mid = (mass - hi).astype(BF16).astype(F32)
        low = mass - hi - mid
        packed = jnp.where(lane == 3 * s, hi, jnp.where(lane == 3 * s + 1, mid, jnp.where(lane == 3 * s + 2, low, 0.0)))
        send, recv = (rs_send, rs_recv) if t == 0 else (rz_send.at[t - 1], rz_recv.at[t - 1])
        for c in range(DB):
            part = arrived[c * PN:(c + 1) * PN]
            at = slice((c % BPZ) * B, (c % BPZ + 1) * B)
            arr[c // BPZ, :, at] = part
            send[c // BPZ, :, at] = part.astype(send.dtype)
        for c in range(S):
            send[c, :, W:W + LANES] = packed.astype(send.dtype)
        copies = [start(to_src(send.at[src_peers[r]], recv.at[r - 1], rs_ss.at[t, r - 1], rs_rs.at[t, r - 1], r))
                  for r in range(1, S)]
        return copies, recv, packed.astype(BF16).astype(F32)

    def owned(pushed):
        copies, recv, packed = pushed
        raw = arr[s]
        for r in range(1, S):
            copies[r - 1].wait_recv()
            raw = raw + recv[r - 1, :, :W].astype(F32)
            packed = packed + recv[r - 1, :, W:W + LANES].astype(F32)
        return raw, packed

    def scale_of(packed):
        mass = jnp.sum(packed, axis=1, keepdims=True)
        return N / mass

    def weigh(block, raw, scale):
        now = raw * scale
        wbuf[0, block] = (pol[0, block] * now).astype(BF16)
        wbuf[1, block] = (pol[1, block] * now).astype(BF16)

    def share_density(t, raw, packed):
        ag_send[t, :, :W] = raw.astype(BF16)
        ag_send[t, :, W:W + LANES] = packed.astype(BF16)
        return share(2 + t, ag_send.at[t], lambda r: ag_recv.at[t, r])

    def take_density(t, raw, packed, shared):
        slot = lambda r: ag_recv.at[t, r]
        relay(2 + t, shared, slot, lambda r: ag_recv.at[t, Z + r])
        for i in range(1, 2 * Z):
            packed = packed + ag_recv[t, i, :, W:W + LANES].astype(F32)
        scale = scale_of(packed)
        for b in range(BPZ):
            weigh(BPZ * d + b, raw[:, b * B:(b + 1) * B], scale)
        for i in range(1, 2 * Z):
            for b in range(BPZ):
                weigh(BPZ * came_from(i) + b, ag_recv[t, i, :, b * B:(b + 1) * B].astype(F32), scale)
        return raw * scale

    def send_mass(i, packed):
        ms_send[i] = packed.astype(BF16)
        return [start(to_dst(ms_send.at[i], ms_recv.at[i, r - 1], ms_ss.at[i, r - 1], ms_rs.at[i, r - 1], r))
                for r in range(1, D)]

    def take_mass(i, packed, copies):
        for r in range(1, D):
            copies[r - 1].wait_recv()
            packed = packed + ms_recv[i, r - 1].astype(F32)
        return scale_of(packed)

    def collect(a, block):
        out = None
        for k in range(K):
            term = jnp.where(tile_src[0, 0, a, k] == block, 1.0, 0.0).astype(F32) * prod[a * K + k]
            out = term if out is None else out + term
        return out

    def parts(t, block):
        out = [collect(a, block) for a in range(A)]
        return out if t == 0 else [pol[0, block] * out[0] + pol[1, block] * out[1]]

    order = list(range(1, Z)) + [0]

    def pull(t):
        for copy in va[t]:
            copy.wait_recv()
        for a in range(A):
            for k in range(K):
                q = a * K + k
                v = vbuf[t][tile_dst[0, 0, a, k]]
                live = jnp.where(k < tile_count[0, 0, a], 1.0, 0.0).astype(F32)
                prod[q] = live * lax.dot_general(
                    v, tiles[q * B:(q + 1) * B, :], (((1,), (1,)), ((), ())), preferred_element_type=F32)
        n = A * BPZ if t == 0 else BPZ
        copies = {}
        for r in order:
            for b in range(BPZ):
                for i, part in enumerate(parts(t, BPZ * (2 * z_peers[r] + 1 - core) + b)):
                    pr_send[t, r, i * BPZ + b] = part
            copies[r] = start(to_pair(pr_send.at[t, r, pl.ds(0, n)], pr_recv.at[t, r, pl.ds(0, n)],
                                      pr_ss.at[t, r], pr_rs.at[t, r]))
        for r in order:
            for b in range(BPZ):
                for i, part in enumerate(parts(t, BPZ * (2 * z_peers[r] + core) + b)):
                    keep[t, r, i * BPZ + b] = part
        return copies

    def spread(t, copies):
        n = A * BPZ if t == 0 else BPZ
        send, recv = (zl_send, zl_recv) if t == 0 else (zs_send.at[t - 1], zs_recv.at[t - 1])
        out = []
        for r in order:
            copies[r].wait_recv()
            for m in range(n):
                both = keep[t, r, m] + pr_recv[t, r, m]
                if r == 0:
                    keep[t, r, m] = both
                else:
                    send[r - 1, m] = both.astype(send.dtype)
            if r:
                out.append(start(to_z(send.at[r - 1], recv.at[r - 1], zs_ss.at[t, r - 1], zs_rs.at[t, r - 1], r)))
        return out

    def summed(t, m):
        recv = zl_recv if t == 0 else zs_recv.at[t - 1]
        total = keep[t, 0, m]
        for r in range(1, Z):
            total = total + recv[r - 1, m].astype(F32)
        return total

    def crowding(t, now):
        own[t] = own[4] * jnp.log(1.0 + jnp.mean(now, axis=0, keepdims=True))

    def next_value(t, copies):
        reward = []
        for b in range(BPZ):
            cols = slice(b * B, (b + 1) * B)
            q0, q1 = own[5, :, cols], own[6, :, cols]
            reward.append(q0 * base_reward[0, :, cols] + q1 * base_reward[1, :, cols] - (q0 + q1) * own[t, :, cols])
        for copy in copies:
            copy.wait_recv()
        for b in range(BPZ):
            vbuf[t - 1][BPZ * s + b] = (reward[b] + DISCOUNT * summed(t, b)).astype(BF16)
        va[t - 1] = share_value(t - 1)

    relay(0, w0, w0_here, w0_here)
    mg_mine = margin.at[blocks_of(d)]
    mg_here = lambda r: margin.at[blocks_of(2 * z_back[r] + core)]
    mg = share(1, mg_mine, lambda r: mg_mine)
    for load in loads[7:]:
        load.wait()
    pushed = push(0)
    crowding(0, rho)
    relay(1, mg, mg_here, mg_here)

    def policy(g, _):
        for b in range(BPZ):
            c = g * BPZ + b
            pol[0, c] = jax.nn.sigmoid(margin[c])
            pol[1, c] = jax.nn.sigmoid(-margin[c])
        return _

    lax.fori_loop(0, D, policy, 0)
    raw, packed = owned(pushed)
    shared = share_density(0, raw, packed)
    now = take_density(0, raw, packed, shared)
    pushed = push(1)
    crowding(1, now)
    pr = pull(3)
    raw, packed = owned(pushed)
    shared = share_density(1, raw, packed)
    now = take_density(1, raw, packed, shared)
    pushed = push(2)
    crowding(2, now)
    zs = spread(3, pr)
    raw, packed = owned(pushed)
    ms = send_mass(0, packed)
    ag3_send[...] = raw
    scale3 = take_mass(0, packed, ms)
    now = raw * scale3
    crowding(3, now)
    next_value(3, zs)
    shared = share(4, ag3_send, lambda r: ag3_recv.at[r])
    pr = pull(2)
    zs = spread(2, pr)
    relay(4, shared, lambda r: ag3_recv.at[r], lambda r: ag3_recv.at[Z + r])
    for b in range(BPZ):
        weigh(BPZ * d + b, raw[:, b * B:(b + 1) * B], scale3)
        for i in range(1, 2 * Z):
            weigh(BPZ * came_from(i) + b, ag3_recv[i, :, b * B:(b + 1) * B], scale3)
    next_value(2, zs)
    pushed = push(3)
    pr = pull(1)
    zs = spread(1, pr)
    raw, packed = owned(pushed)
    ms = send_mass(1, packed)
    next_value(1, zs)
    result[A + 1] = raw * take_mass(1, packed, ms)
    pr = pull(0)
    zs = spread(0, pr)
    for copy in zs:
        copy.wait_recv()
    for b in range(BPZ):
        cols = slice(b * B, (b + 1) * B)
        value = None
        for a in range(A):
            action_value = base_reward[a, :, cols] - own[0, :, cols] + DISCOUNT * summed(0, a * BPZ + b)
            result[a, :, cols] = logits[a, :, cols] + STEP_SIZE * action_value
            term = own[5 + a, :, cols] * action_value
            value = term if value is None else value + term
        result[A, :, cols] = value
    for copy in pending:
        copy.wait_send()


def body(density0, logits, value_final, base_reward, crowd, tiles, tile_src, tile_dst, tile_count):
    S, D = lax.axis_size("src"), lax.axis_size("dst")
    PN, W = density0.shape
    A, K, B = tiles.shape[2], tiles.shape[3], tiles.shape[-1]
    BPZ = W // B
    SB, DB, Z = BPZ * D, BPZ * S, D // 2
    N = float(W * S * D)
    dma = pltpu.SemaphoreType.DMA
    V = pltpu.VMEM
    args = (density0, logits, value_final, base_reward, crowd, tiles.reshape(A * K * B, B), tile_src, tile_dst, tile_count)
    places = (V, V, V, V, pltpu.SMEM, V, pltpu.SMEM, pltpu.SMEM, pltpu.SMEM)
    shared = dma((5, 2 * Z - 1))
    scratch = [place(x.shape, x.dtype) for place, x in zip(places, args)] + [
        dma((len(args),)),
        V((A, SB, PN, B), BF16), V((A, SB, PN, B), BF16), V((A, SB, PN, B), F32), V((SB, PN, B), F32),
        V((DB * PN, A * K * B), BF16), V((A * K * DB, PN, LANES), BF16), V((A * K, PN, B), F32), V((S, PN, W), F32),
        V((S, PN, W + LANES), BF16), V((S - 1, PN, W + LANES), BF16),
        V((H - 1, S, PN, W + LANES), F32), V((H - 1, S - 1, PN, W + LANES), F32),
        V((2, PN, W + LANES), BF16), V((2, 2 * Z, PN, W + LANES), BF16),
        V((PN, W), F32), V((2 * Z, PN, W), F32), V((2, PN, LANES), BF16), V((2, D - 1, PN, LANES), BF16),
        *[V((DB, PN, B), BF16)] * H,
        V((H, Z, A * BPZ, PN, B), F32), V((H, Z, A * BPZ, PN, B), F32),
        V((H - 1, Z - 1, BPZ, PN, B), BF16), V((H - 1, Z - 1, BPZ, PN, B), BF16),
        V((Z - 1, A * BPZ, PN, B), F32), V((Z - 1, A * BPZ, PN, B), F32),
        V((H, Z, A * BPZ, PN, B), F32), V((7, PN, W), F32),
        dma((H, S - 1)), dma((H, S - 1)), shared, shared, dma((2, D - 1)), dma((2, D - 1)),
        dma((H, S - 1)), dma((H, S - 1)), dma((H, Z)), dma((H, Z)), dma((H, Z - 1)), dma((H, Z - 1)),
    ]
    flops = 2 * H * 2 * A * K * PN * B * B
    out = pl.pallas_call(
        functools.partial(kernel, S, D, N, B, BPZ, A, K),
        out_shape=jax.ShapeDtypeStruct((A + 2, PN, W), F32),
        in_specs=[pl.BlockSpec(memory_space=pltpu.HBM)] * len(args),
        out_specs=pl.BlockSpec(memory_space=pltpu.VMEM),
        scratch_shapes=scratch,
        cost_estimate=pl.CostEstimate(flops=flops, bytes_accessed=tiles.size * 2, transcendentals=0),
        compiler_params=pltpu.CompilerParams(
            collective_id=0, has_side_effects=True, vmem_limit_bytes=62 * 1024 * 1024),
    )(*args)
    return out[:A], out[A], out[A + 1]


def solution(mesh):
    in_specs = (
        P(None, ("src", "dst")),
        P(None, None, ("src", "dst")),
        P(None, ("src", "dst")),
        P(None, None, ("src", "dst")),
        P(),
        P("src", "dst", None, None, None, None),
        P("src", "dst", None, None),
        P("src", "dst", None, None),
        P("src", "dst", None),
    )
    out_specs = (P(None, None, ("src", "dst")), P(None, ("src", "dst")), P(None, ("src", "dst")))
    return jax.shard_map(body, mesh=mesh, in_specs=in_specs, out_specs=out_specs, check_vma=False)
```

```python
import functools

import jax
import jax.numpy as jnp
from jax import lax
from jax.experimental import pallas as pl
from jax.experimental.pallas import tpu as pltpu
from jax.sharding import PartitionSpec as P

H = 4
LANES = 128
DISCOUNT = 0.9
STEP_SIZE = 1.0
MESH = pl.DeviceIdType.MESH
F32 = jnp.float32
BF16 = jnp.bfloat16


def kernel(
    S, D, N, B, BPZ, A, K,
    density0_h, logits_h, value_final_h, base_reward_h, crowd_h, tiles_h, tile_src_h, tile_dst_h, tile_count_h,
    result,
    density0, logits, value_final, base_reward, crowd, tiles, tile_src, tile_dst, tile_count, in_sem,
    turned, wbuf, w0buf, pol, margin, lhs, mask, prod, arr,
    rs_send, rs_recv, rz_send, rz_recv, ag_send, ag_recv, ag3_send, ag3_recv, ms_send, ms_recv,
    vb0, vb1, vb2, vb3, pr_send, pr_recv, zs_send, zs_recv, zl_send, zl_recv, zh_send, zh_recv, keep, own,
    rs_ss, rs_rs, sh_ss, sh_rs, ms_ss, ms_rs, va_ss, va_rs, pr_ss, pr_rs, zs_ss, zs_rs,
):
    vbuf = (vb0, vb1, vb2, vb3)
    s = lax.axis_index("src")
    d = lax.axis_index("dst")
    Z = D // 2
    z = d // 2
    core = d - 2 * z
    PN, W = density0.shape
    src_peers = [lax.rem(s + r, S) for r in range(S)]
    dst_peers = [lax.rem(d + r, D) for r in range(D)]
    z_peers = [lax.rem(z + r, Z) for r in range(Z)]
    z_back = [lax.rem(z + Z - r, Z) for r in range(Z)]

    def remote(src, dst, ss, rs, device):
        return pltpu.make_async_remote_copy(
            src_ref=src, dst_ref=dst, send_sem=ss, recv_sem=rs, device_id=device, device_id_type=MESH)

    def to_src(src, dst, ss, rs, r):
        return remote(src, dst, ss, rs, (src_peers[r], d))

    def to_dst(src, dst, ss, rs, r):
        return remote(src, dst, ss, rs, (s, dst_peers[r]))

    def to_z(src, dst, ss, rs, r):
        return remote(src, dst, ss, rs, (s, 2 * z_peers[r] + core))

    def to_pair(src, dst, ss, rs):
        return remote(src, dst, ss, rs, (s, 2 * z + 1 - core))

    loads = [pltpu.make_async_copy(h, v, in_sem.at[i]) for i, (h, v) in enumerate((
        (logits_h, logits), (density0_h, density0), (value_final_h, value_final), (tile_src_h, tile_src),
        (tile_dst_h, tile_dst), (tile_count_h, tile_count), (crowd_h, crowd), (base_reward_h, base_reward),
        (tiles_h, tiles)))]
    for load in loads:
        load.start()
    barrier = pltpu.get_barrier_semaphore()
    for r in range(1, S):
        pl.semaphore_signal(barrier, inc=1, device_id=(src_peers[r], d), device_id_type=MESH)
    for r in range(1, D):
        pl.semaphore_signal(barrier, inc=1, device_id=(s, dst_peers[r]), device_id_type=MESH)

    for load in loads[:3]:
        load.wait()
    gap = logits[0] - logits[1]
    p0, p1 = jax.nn.sigmoid(gap), jax.nn.sigmoid(-gap)
    rho = density0[...]
    vf = value_final[...].astype(BF16)
    for b in range(BPZ):
        cols = slice(b * B, (b + 1) * B)
        w0buf[0, BPZ * d + b] = (p0 * rho)[:, cols].astype(BF16)
        w0buf[1, BPZ * d + b] = (p1 * rho)[:, cols].astype(BF16)
        margin[BPZ * d + b] = gap[:, cols]
        vbuf[3][BPZ * s + b] = vf[:, cols]
    pl.semaphore_wait(barrier, S + D - 2)

    pending = []

    def start(copy):
        copy.start()
        pending.append(copy)
        return copy

    def share(i, own_ref, there):
        ss, rs = sh_ss.at[i], sh_rs.at[i]
        hops = [start(to_z(own_ref, there(r), ss.at[r - 1], rs.at[r - 1], r)) for r in range(1, Z)]
        return hops, start(to_pair(own_ref, there(Z), ss.at[Z - 1], rs.at[Z - 1]))

    def relay(i, shared, here, there):
        ss, rs = sh_ss.at[i], sh_rs.at[i]
        hops, pair = shared
        onward = []
        for r in range(1, Z):
            hops[r - 1].wait_recv()
            onward.append(start(to_pair(here(r), there(r), ss.at[Z - 1 + r], rs.at[Z - 1 + r])))
        pair.wait_recv()
        for copy in onward:
            copy.wait_recv()

    def blocks_of(j):
        return pl.ds(BPZ * j, BPZ)

    def came_from(i):
        return 2 * z_back[i % Z] + (core if i < Z else 1 - core)

    def share_value(t):
        at = vbuf[t].at[pl.ds(BPZ * s, BPZ)]
        return [start(to_src(at, at, va_ss.at[t, r - 1], va_rs.at[t, r - 1], r)) for r in range(1, S)]

    w0_mine = w0buf.at[:, blocks_of(d)]
    w0_here = lambda r: w0buf.at[:, blocks_of(2 * z_back[r] + core)]
    w0 = share(0, w0_mine, lambda r: w0_mine)
    va = {3: share_value(3)}

    for load in loads[3:7]:
        load.wait()
    for a in range(A):
        for k in range(K):
            live = jnp.where(k < tile_count[0, 0, a], 1.0, 0.0).astype(F32)
            for c in range(BPZ * S):
                hit = jnp.where(tile_dst[0, 0, a, k] == c, live, 0.0)
                mask[(a * K + k) * BPZ * S + c] = jnp.full((PN, LANES), hit, F32).astype(BF16)
    row = lax.broadcasted_iota(jnp.int32, (PN, W), 0)
    crowd_col = jnp.zeros((PN, W), F32)
    for p in range(PN):
        crowd_col = jnp.where(row == p, crowd[p], crowd_col)
    own[4] = crowd_col
    own[5] = p0
    own[6] = p1
    lane = lax.broadcasted_iota(jnp.int32, (PN, LANES), 1)
    DB = BPZ * S

    def push(t):
        for a in range(A):
            for k in range(K):
                w = (w0buf if t == 0 else wbuf)[a, tile_src[0, 0, a, k]]
                q = a * K + k
                for c in range(DB):
                    m = mask[q * DB + c]
                    lhs[c * PN:(c + 1) * PN, q * B:(q + 1) * B] = w * jnp.concatenate([m] * (B // LANES), axis=1)
        arrived = jnp.dot(lhs[...], tiles[...], preferred_element_type=F32)
        total = arrived[0:PN]
        for c in range(1, DB):
            total = total + arrived[c * PN:(c + 1) * PN]
        mass = jnp.broadcast_to(jnp.sum(total, axis=1, keepdims=True), (PN, LANES))
        hi = mass.astype(BF16).astype(F32)
        mid = (mass - hi).astype(BF16).astype(F32)
        low = mass - hi - mid
        packed = jnp.where(lane == 3 * s, hi, jnp.where(lane == 3 * s + 1, mid, jnp.where(lane == 3 * s + 2, low, 0.0)))
        send, recv = (rs_send.at[t], rs_recv.at[t]) if t < 2 else (rz_send.at[t - 2], rz_recv.at[t - 2])
        for c in range(DB):
            part = arrived[c * PN:(c + 1) * PN]
            at = slice((c % BPZ) * B, (c % BPZ + 1) * B)
            arr[c // BPZ, :, at] = part
            send[c // BPZ, :, at] = part.astype(send.dtype)
        for c in range(S):
            send[c, :, W:W + LANES] = packed.astype(send.dtype)
        copies = [start(to_src(send.at[src_peers[r]], recv.at[r - 1], rs_ss.at[t, r - 1], rs_rs.at[t, r - 1], r))
                  for r in range(1, S)]
        return copies, recv, packed.astype(BF16).astype(F32)

    def owned(pushed):
        copies, recv, packed = pushed
        raw = arr[s]
        for r in range(1, S):
            copies[r - 1].wait_recv()
            raw = raw + recv[r - 1, :, :W].astype(F32)
            packed = packed + recv[r - 1, :, W:W + LANES].astype(F32)
        return raw, packed

    def scale_of(packed):
        mass = jnp.sum(packed, axis=1, keepdims=True)
        return N / mass

    def weigh(block, raw, scale):
        now = raw * scale
        wbuf[0, block] = (pol[0, block] * now).astype(BF16)
        wbuf[1, block] = (pol[1, block] * now).astype(BF16)

    def share_density(t, raw, packed):
        ag_send[t, :, :W] = raw.astype(BF16)
        ag_send[t, :, W:W + LANES] = packed.astype(BF16)
        return share(2 + t, ag_send.at[t], lambda r: ag_recv.at[t, r])

    def take_density(t, raw, packed, shared):
        slot = lambda r: ag_recv.at[t, r]
        relay(2 + t, shared, slot, lambda r: ag_recv.at[t, Z + r])
        for i in range(1, 2 * Z):
            packed = packed + ag_recv[t, i, :, W:W + LANES].astype(F32)
        scale = scale_of(packed)
        for b in range(BPZ):
            weigh(BPZ * d + b, raw[:, b * B:(b + 1) * B], scale)
        for i in range(1, 2 * Z):
            for b in range(BPZ):
                weigh(BPZ * came_from(i) + b, ag_recv[t, i, :, b * B:(b + 1) * B].astype(F32), scale)
        return raw * scale

    def send_mass(i, packed):
        ms_send[i] = packed.astype(BF16)
        return [start(to_dst(ms_send.at[i], ms_recv.at[i, r - 1], ms_ss.at[i, r - 1], ms_rs.at[i, r - 1], r))
                for r in range(1, D)]

    def take_mass(i, packed, copies):
        for r in range(1, D):
            copies[r - 1].wait_recv()
            packed = packed + ms_recv[i, r - 1].astype(F32)
        return scale_of(packed)

    def collect(a, block):
        out = None
        for k in range(K):
            term = jnp.where(tile_src[0, 0, a, k] == block, 1.0, 0.0).astype(F32) * prod[a * K + k]
            out = term if out is None else out + term
        return out

    def parts(t, block):
        out = [collect(a, block) for a in range(A)]
        return out if t == 0 else [pol[0, block] * out[0] + pol[1, block] * out[1]]

    order = list(range(1, Z)) + [0]

    def pull(t):
        for copy in va[t]:
            copy.wait_recv()
        for a in range(A):
            for k in range(K):
                q = a * K + k
                v = vbuf[t][tile_dst[0, 0, a, k]]
                live = jnp.where(k < tile_count[0, 0, a], 1.0, 0.0).astype(F32)
                prod[q] = live * jnp.dot(v, turned[q * B:(q + 1) * B, :], preferred_element_type=F32)
        n = A * BPZ if t == 0 else BPZ
        copies = {}
        for r in order:
            for b in range(BPZ):
                for i, part in enumerate(parts(t, BPZ * (2 * z_peers[r] + 1 - core) + b)):
                    pr_send[t, r, i * BPZ + b] = part
            copies[r] = start(to_pair(pr_send.at[t, r, pl.ds(0, n)], pr_recv.at[t, r, pl.ds(0, n)],
                                      pr_ss.at[t, r], pr_rs.at[t, r]))
        for r in order:
            for b in range(BPZ):
                for i, part in enumerate(parts(t, BPZ * (2 * z_peers[r] + core) + b)):
                    keep[t, r, i * BPZ + b] = part
        return copies

    def spread(t, copies):
        n = A * BPZ if t == 0 else BPZ
        sends = last_sends if t == 0 else [(zs_send.at[t - 1], zs_recv.at[t - 1], t)]
        out = []
        for r in order:
            copies[r].wait_recv()
            for m in range(n):
                both = keep[t, r, m] + pr_recv[t, r, m]
                if r == 0:
                    keep[t, r, m] = both
                else:
                    i, at = last_place(m) if t == 0 else (0, m)
                    sends[i][0][r - 1, at] = both.astype(sends[i][0].dtype)
            if r:
                for send, recv, row in sends:
                    out.append(start(to_z(send.at[r - 1], recv.at[r - 1], zs_ss.at[row, r - 1], zs_rs.at[row, r - 1], r)))
        return out

    last_sends = [(zl_send, zl_recv, 0), (zh_send, zh_recv, H)]

    def last_place(m):
        a, b = m // BPZ, m % BPZ
        return b % 2, a * (BPZ // 2 if b % 2 else BPZ - BPZ // 2) + b // 2

    def summed(t, m):
        i, at = last_place(m) if t == 0 else (0, m)
        recv = last_sends[i][1] if t == 0 else zs_recv.at[t - 1]
        total = keep[t, 0, m]
        for r in range(1, Z):
            total = total + recv[r - 1, at].astype(F32)
        return total

    def crowding(t, now):
        own[t] = own[4] * jnp.log(1.0 + jnp.mean(now, axis=0, keepdims=True))

    def next_value(t, copies):
        reward = []
        for b in range(BPZ):
            cols = slice(b * B, (b + 1) * B)
            q0, q1 = own[5, :, cols], own[6, :, cols]
            reward.append(q0 * base_reward[0, :, cols] + q1 * base_reward[1, :, cols] - (q0 + q1) * own[t, :, cols])
        for copy in copies:
            copy.wait_recv()
        for b in range(BPZ):
            vbuf[t - 1][BPZ * s + b] = (reward[b] + DISCOUNT * summed(t, b)).astype(BF16)
        va[t - 1] = share_value(t - 1)

    for load in loads[7:]:
        load.wait()

    def turn(q, _):
        at = pl.ds(pl.multiple_of(q * B, B), B)
        turned[at, :] = tiles[at, :].T
        return _

    lax.fori_loop(0, A * K, turn, 0)
    relay(0, w0, w0_here, w0_here)
    mg_mine = margin.at[blocks_of(d)]
    mg_here = lambda r: margin.at[blocks_of(2 * z_back[r] + core)]
    mg = share(1, mg_mine, lambda r: mg_mine)
    pushed = push(0)
    crowding(0, rho)
    relay(1, mg, mg_here, mg_here)

    def policy(g, _):
        for b in range(BPZ):
            c = g * BPZ + b
            pol[0, c] = jax.nn.sigmoid(margin[c])
            pol[1, c] = jax.nn.sigmoid(-margin[c])
        return _

    lax.fori_loop(0, D, policy, 0)
    raw, packed = owned(pushed)
    shared = share_density(0, raw, packed)
    now = take_density(0, raw, packed, shared)
    pushed = push(1)
    crowding(1, now)
    pr = pull(3)
    raw, packed = owned(pushed)
    shared = share_density(1, raw, packed)
    now = take_density(1, raw, packed, shared)
    pushed = push(2)
    crowding(2, now)
    zs = spread(3, pr)
    raw, packed = owned(pushed)
    ms = send_mass(0, packed)
    ag3_send[...] = raw
    scale3 = take_mass(0, packed, ms)
    now = raw * scale3
    crowding(3, now)
    next_value(3, zs)
    shared = share(4, ag3_send, lambda r: ag3_recv.at[r])
    pr = pull(2)
    zs = spread(2, pr)
    relay(4, shared, lambda r: ag3_recv.at[r], lambda r: ag3_recv.at[Z + r])
    for b in range(BPZ):
        weigh(BPZ * d + b, raw[:, b * B:(b + 1) * B], scale3)
        for i in range(1, 2 * Z):
            weigh(BPZ * came_from(i) + b, ag3_recv[i, :, b * B:(b + 1) * B], scale3)
    next_value(2, zs)
    pushed = push(3)
    pr = pull(1)
    zs = spread(1, pr)
    raw, packed = owned(pushed)
    ms = send_mass(1, packed)
    next_value(1, zs)
    result[A + 1] = raw * take_mass(1, packed, ms)
    pr = pull(0)
    zs = spread(0, pr)
    for copy in zs:
        copy.wait_recv()
    for b in range(BPZ):
        cols = slice(b * B, (b + 1) * B)
        value = None
        for a in range(A):
            action_value = base_reward[a, :, cols] - own[0, :, cols] + DISCOUNT * summed(0, a * BPZ + b)
            result[a, :, cols] = logits[a, :, cols] + STEP_SIZE * action_value
            term = own[5 + a, :, cols] * action_value
            value = term if value is None else value + term
        result[A, :, cols] = value
    for copy in pending:
        copy.wait_send()


def deliver(A, result, new_logits, value_start, density_final, sem):
    parts = ((result.at[pl.ds(0, A)], new_logits), (result.at[A], value_start), (result.at[A + 1], density_final))
    copies = [pltpu.make_async_copy(part, out, sem.at[i]) for i, (part, out) in enumerate(parts)]
    for copy in copies:
        copy.start()
    for copy in copies:
        copy.wait()


def body(density0, logits, value_final, base_reward, crowd, tiles, tile_src, tile_dst, tile_count):
    S, D = lax.axis_size("src"), lax.axis_size("dst")
    PN, W = density0.shape
    A, K, B = tiles.shape[2], tiles.shape[3], tiles.shape[-1]
    BPZ = W // B
    SB, DB, Z = BPZ * D, BPZ * S, D // 2
    N = float(W * S * D)
    dma = pltpu.SemaphoreType.DMA
    V = pltpu.VMEM
    args = (density0, logits, value_final, base_reward, crowd, tiles.reshape(A * K * B, B), tile_src, tile_dst, tile_count)
    places = (V, V, V, V, pltpu.SMEM, V, pltpu.SMEM, pltpu.SMEM, pltpu.SMEM)
    shared = dma((5, 2 * Z - 1))
    scratch = [place(x.shape, x.dtype) for place, x in zip(places, args)] + [
        dma((len(args),)), V((A * K * B, B), BF16),
        V((A, SB, PN, B), BF16), V((A, SB, PN, B), BF16), V((A, SB, PN, B), F32), V((SB, PN, B), F32),
        V((DB * PN, A * K * B), BF16), V((A * K * DB, PN, LANES), BF16), V((A * K, PN, B), F32), V((S, PN, W), F32),
        V((2, S, PN, W + LANES), BF16), V((2, S - 1, PN, W + LANES), BF16),
        V((H - 2, S, PN, W + LANES), F32), V((H - 2, S - 1, PN, W + LANES), F32),
        V((2, PN, W + LANES), BF16), V((2, 2 * Z, PN, W + LANES), BF16),
        V((PN, W), F32), V((2 * Z, PN, W), F32), V((2, PN, LANES), BF16), V((2, D - 1, PN, LANES), BF16),
        *[V((DB, PN, B), BF16)] * H,
        V((H, Z, A * BPZ, PN, B), F32), V((H, Z, A * BPZ, PN, B), F32),
        V((H - 1, Z - 1, BPZ, PN, B), BF16), V((H - 1, Z - 1, BPZ, PN, B), BF16),
        V((Z - 1, A * (BPZ - BPZ // 2), PN, B), F32), V((Z - 1, A * (BPZ - BPZ // 2), PN, B), F32),
        V((Z - 1, A * (BPZ // 2), PN, B), BF16), V((Z - 1, A * (BPZ // 2), PN, B), BF16),
        V((H, Z, A * BPZ, PN, B), F32), V((7, PN, W), F32),
        dma((H, S - 1)), dma((H, S - 1)), shared, shared, dma((2, D - 1)), dma((2, D - 1)),
        dma((H, S - 1)), dma((H, S - 1)), dma((H, Z)), dma((H, Z)), dma((H + 1, Z - 1)), dma((H + 1, Z - 1)),
    ]
    flops = 2 * H * 2 * A * K * PN * B * B
    out = pl.pallas_call(
        functools.partial(kernel, S, D, N, B, BPZ, A, K),
        out_shape=jax.ShapeDtypeStruct((A + 2, PN, W), F32),
        in_specs=[pl.BlockSpec(memory_space=pltpu.HBM)] * len(args),
        out_specs=pl.BlockSpec(memory_space=pltpu.VMEM),
        scratch_shapes=scratch,
        cost_estimate=pl.CostEstimate(flops=flops, bytes_accessed=tiles.size * 2, transcendentals=0),
        compiler_params=pltpu.CompilerParams(
            collective_id=0, has_side_effects=True, vmem_limit_bytes=62 * 1024 * 1024),
    )(*args)
    hbm = pl.BlockSpec(memory_space=pltpu.HBM)
    return pl.pallas_call(
        functools.partial(deliver, A),
        out_shape=(jax.ShapeDtypeStruct((A, PN, W), F32),) + (jax.ShapeDtypeStruct((PN, W), F32),) * 2,
        in_specs=[hbm],
        out_specs=(hbm,) * 3,
        scratch_shapes=[dma((3,))],
        compiler_params=pltpu.CompilerParams(vmem_limit_bytes=62 * 1024 * 1024),
    )(out)


def solution(mesh):
    in_specs = (
        P(None, ("src", "dst")),
        P(None, None, ("src", "dst")),
        P(None, ("src", "dst")),
        P(None, None, ("src", "dst")),
        P(),
        P("src", "dst", None, None, None, None),
        P("src", "dst", None, None),
        P("src", "dst", None, None),
        P("src", "dst", None),
    )
    out_specs = (P(None, None, ("src", "dst")), P(None, ("src", "dst")), P(None, ("src", "dst")))
    return jax.shard_map(body, mesh=mesh, in_specs=in_specs, out_specs=out_specs, check_vma=False)
```

```python
import functools

import jax
import jax.numpy as jnp
from jax import lax
from jax.experimental import pallas as pl
from jax.experimental.pallas import tpu as pltpu
from jax.sharding import PartitionSpec as P

H = 4
LANES = 128
DISCOUNT = 0.9
STEP_SIZE = 1.0
MESH = pl.DeviceIdType.MESH
F32 = jnp.float32
BF16 = jnp.bfloat16


def kernel(
    S, D, N, B, BPZ, A, K,
    density0_h, logits_h, value_final_h, base_reward_h, crowd_h, tiles_h, tile_src_h, tile_dst_h, tile_count_h,
    result,
    density0, logits, value_final, base_reward, crowd, tiles, tile_src, tile_dst, tile_count, in_sem,
    turned, wbuf, w0buf, pol, margin, lhs, mask, prod, arr,
    rs_send, rs_recv, rz_send, rz_recv, ag_send, ag_recv, ag3_send, ag3_recv, ms_send, ms_recv,
    vb0, vb1, vb2, vb3, pr_send, pr_recv, zs_send, zs_recv, zl_send, zl_recv, zh_send, zh_recv, row_send, row_recv, col_send, col_recv, keep, own,
    rs_ss, rs_rs, sh_ss, sh_rs, ms_ss, ms_rs, va_ss, va_rs, pr_ss, pr_rs, zs_ss, zs_rs, row_ss, row_rs, col_ss, col_rs,
):
    vbuf = (vb0, vb1, vb2, vb3)
    s = lax.axis_index("src")
    d = lax.axis_index("dst")
    Z = D // 2
    z = d // 2
    core = d - 2 * z
    PN, W = density0.shape
    src_peers = [lax.rem(s + r, S) for r in range(S)]
    dst_peers = [lax.rem(d + r, D) for r in range(D)]
    z_peers = [lax.rem(z + r, Z) for r in range(Z)]
    z_back = [lax.rem(z + Z - r, Z) for r in range(Z)]

    def remote(src, dst, ss, rs, device):
        return pltpu.make_async_remote_copy(
            src_ref=src, dst_ref=dst, send_sem=ss, recv_sem=rs, device_id=device, device_id_type=MESH)

    def to_src(src, dst, ss, rs, r):
        return remote(src, dst, ss, rs, (src_peers[r], d))

    def to_dst(src, dst, ss, rs, r):
        return remote(src, dst, ss, rs, (s, dst_peers[r]))

    def to_z(src, dst, ss, rs, r):
        return remote(src, dst, ss, rs, (s, 2 * z_peers[r] + core))

    def to_pair(src, dst, ss, rs):
        return remote(src, dst, ss, rs, (s, 2 * z + 1 - core))

    loads = [pltpu.make_async_copy(h, v, in_sem.at[i]) for i, (h, v) in enumerate((
        (logits_h, logits), (density0_h, density0), (value_final_h, value_final), (tile_src_h, tile_src),
        (tile_dst_h, tile_dst), (tile_count_h, tile_count), (crowd_h, crowd), (base_reward_h, base_reward),
        (tiles_h, tiles)))]
    for load in loads:
        load.start()
    barrier = pltpu.get_barrier_semaphore()
    for r in range(1, S):
        pl.semaphore_signal(barrier, inc=1, device_id=(src_peers[r], d), device_id_type=MESH)
    for r in range(1, D):
        pl.semaphore_signal(barrier, inc=1, device_id=(s, dst_peers[r]), device_id_type=MESH)

    for load in loads[:3]:
        load.wait()
    gap = logits[0] - logits[1]
    p0, p1 = jax.nn.sigmoid(gap), jax.nn.sigmoid(-gap)
    rho = density0[...]
    vf = value_final[...].astype(BF16)
    for b in range(BPZ):
        cols = slice(b * B, (b + 1) * B)
        w0buf[0, BPZ * d + b] = (p0 * rho)[:, cols].astype(BF16)
        w0buf[1, BPZ * d + b] = (p1 * rho)[:, cols].astype(BF16)
        margin[BPZ * d + b] = gap[:, cols]
        vbuf[3][BPZ * s + b] = vf[:, cols]
    pl.semaphore_wait(barrier, S + D - 2)

    pending = []

    def start(copy):
        copy.start()
        pending.append(copy)
        return copy

    def share(i, own_ref, there):
        ss, rs = sh_ss.at[i], sh_rs.at[i]
        hops = [start(to_z(own_ref, there(r), ss.at[r - 1], rs.at[r - 1], r)) for r in range(1, Z)]
        return hops, start(to_pair(own_ref, there(Z), ss.at[Z - 1], rs.at[Z - 1]))

    def relay(i, shared, here, there):
        ss, rs = sh_ss.at[i], sh_rs.at[i]
        hops, pair = shared
        onward = []
        for r in range(1, Z):
            hops[r - 1].wait_recv()
            onward.append(start(to_pair(here(r), there(r), ss.at[Z - 1 + r], rs.at[Z - 1 + r])))
        pair.wait_recv()
        for copy in onward:
            copy.wait_recv()

    def blocks_of(j):
        return pl.ds(BPZ * j, BPZ)

    def came_from(i):
        return 2 * z_back[i % Z] + (core if i < Z else 1 - core)

    def share_value(t):
        at = vbuf[t].at[pl.ds(BPZ * s, BPZ)]
        return [start(to_src(at, at, va_ss.at[t, r - 1], va_rs.at[t, r - 1], r)) for r in range(1, S)]

    w0_mine = w0buf.at[:, blocks_of(d)]
    w0_here = lambda r: w0buf.at[:, blocks_of(2 * z_back[r] + core)]
    w0 = share(0, w0_mine, lambda r: w0_mine)
    va = {3: share_value(3)}

    for load in loads[3:7]:
        load.wait()
    for a in range(A):
        for k in range(K):
            live = jnp.where(k < tile_count[0, 0, a], 1.0, 0.0).astype(F32)
            for c in range(BPZ * S):
                hit = jnp.where(tile_dst[0, 0, a, k] == c, live, 0.0)
                mask[(a * K + k) * BPZ * S + c] = jnp.full((PN, LANES), hit, F32).astype(BF16)
    row = lax.broadcasted_iota(jnp.int32, (PN, W), 0)
    crowd_col = jnp.zeros((PN, W), F32)
    for p in range(PN):
        crowd_col = jnp.where(row == p, crowd[p], crowd_col)
    own[4] = crowd_col
    own[5] = p0
    own[6] = p1
    lane = lax.broadcasted_iota(jnp.int32, (PN, LANES), 1)
    DB = BPZ * S

    def pack(terms):
        mass = jnp.broadcast_to(jnp.sum(terms, axis=1, keepdims=True), (PN, LANES))
        hi = mass.astype(BF16).astype(F32)
        mid = (mass - hi).astype(BF16).astype(F32)
        low = (mass - hi - mid).astype(BF16).astype(F32)
        return jnp.where(lane == 3 * s, hi, jnp.where(lane == 3 * s + 1, mid, jnp.where(lane == 3 * s + 2, low, 0.0)))

    def push(t):
        for a in range(A):
            for k in range(K):
                w = (w0buf if t == 0 else wbuf)[a, tile_src[0, 0, a, k]]
                q = a * K + k
                for c in range(DB):
                    m = mask[q * DB + c]
                    lhs[c * PN:(c + 1) * PN, q * B:(q + 1) * B] = w * jnp.concatenate([m] * (B // LANES), axis=1)
        arrived = jnp.dot(lhs[...], tiles[...], preferred_element_type=F32)
        total = arrived[0:PN]
        for c in range(1, DB):
            total = total + arrived[c * PN:(c + 1) * PN]
        packed = pack(total)
        send, recv = (rs_send.at[t], rs_recv.at[t]) if t < 2 else (rz_send.at[t - 2], rz_recv.at[t - 2])
        for c in range(DB):
            part = arrived[c * PN:(c + 1) * PN]
            at = slice((c % BPZ) * B, (c % BPZ + 1) * B)
            arr[c // BPZ, :, at] = part
            send[c // BPZ, :, at] = part.astype(send.dtype)
        for c in range(S):
            send[c, :, W:W + LANES] = packed.astype(send.dtype)
        copies = [start(to_src(send.at[src_peers[r]], recv.at[r - 1], rs_ss.at[t, r - 1], rs_rs.at[t, r - 1], r))
                  for r in range(1, S)]
        return copies, recv, packed

    def owned(pushed):
        copies, recv, packed = pushed
        raw = arr[s]
        for r in range(1, S):
            copies[r - 1].wait_recv()
            raw = raw + recv[r - 1, :, :W].astype(F32)
            packed = packed + recv[r - 1, :, W:W + LANES].astype(F32)
        return raw, packed

    def scale_of(packed):
        mass = jnp.sum(packed, axis=1, keepdims=True)
        return N / mass

    def weigh(block, raw, scale):
        now = raw * scale
        wbuf[0, block] = (pol[0, block] * now).astype(BF16)
        wbuf[1, block] = (pol[1, block] * now).astype(BF16)

    def share_density(t, raw, packed):
        ag_send[t, :, :W] = raw.astype(BF16)
        ag_send[t, :, W:W + LANES] = packed.astype(BF16)
        return share(2 + t, ag_send.at[t], lambda r: ag_recv.at[t, r])

    def take_density(t, raw, packed, shared):
        slot = lambda r: ag_recv.at[t, r]
        relay(2 + t, shared, slot, lambda r: ag_recv.at[t, Z + r])
        for i in range(1, 2 * Z):
            packed = packed + ag_recv[t, i, :, W:W + LANES].astype(F32)
        scale = scale_of(packed)
        for b in range(BPZ):
            weigh(BPZ * d + b, raw[:, b * B:(b + 1) * B], scale)
        for i in range(1, 2 * Z):
            for b in range(BPZ):
                weigh(BPZ * came_from(i) + b, ag_recv[t, i, :, b * B:(b + 1) * B].astype(F32), scale)
        return raw * scale

    def send_mass(i, packed):
        ms_send[i] = packed.astype(BF16)
        return [start(to_dst(ms_send.at[i], ms_recv.at[i, r - 1], ms_ss.at[i, r - 1], ms_rs.at[i, r - 1], r))
                for r in range(1, D)]

    def take_mass(i, packed, copies):
        for r in range(1, D):
            copies[r - 1].wait_recv()
            packed = packed + ms_recv[i, r - 1].astype(F32)
        return scale_of(packed)

    def collect(a, block):
        out = None
        for k in range(K):
            term = jnp.where(tile_src[0, 0, a, k] == block, 1.0, 0.0).astype(F32) * prod[a * K + k]
            out = term if out is None else out + term
        return out

    def parts(t, block):
        out = [collect(a, block) for a in range(A)]
        return out if t == 0 else [pol[0, block] * out[0] + pol[1, block] * out[1]]

    order = list(range(1, Z)) + [0]

    def row_sums():
        ones = jnp.ones((PN, B), BF16)
        for a in range(A):
            for k in range(K):
                q = a * K + k
                live = jnp.where(k < tile_count[0, 0, a], 1.0, 0.0).astype(F32)
                prod[q] = live * jnp.dot(ones, turned[q * B:(q + 1) * B, :], preferred_element_type=F32)
        rows = row_send.shape[1]
        which = lax.broadcasted_iota(jnp.int32, (rows, B), 0)

        def one(j, _):
            out = jnp.zeros((rows, B), F32)
            for m in range(A * BPZ):
                part = collect(m // BPZ, BPZ * j + m % BPZ)[0:1]
                out = jnp.where(which == m, jnp.broadcast_to(part, (rows, B)), out)
            row_send[j] = out
            return _

        lax.fori_loop(0, D, one, 0)

    def own_mass(now, copies):
        total = row_send[d]
        for r in range(1, D):
            copies[r - 1].wait_recv()
            total = total + row_recv[r - 1]
        terms = jnp.zeros((PN, B), F32)
        for m in range(A * BPZ):
            cols = slice((m % BPZ) * B, (m % BPZ + 1) * B)
            w = (own[5 + m // BPZ, :, cols] * now[:, cols]).astype(BF16).astype(F32)
            terms = terms + w * total[m:m + 1]
        return pack(terms)

    def pull(t):
        for copy in va[t]:
            copy.wait_recv()
        for a in range(A):
            for k in range(K):
                q = a * K + k
                v = vbuf[t][tile_dst[0, 0, a, k]]
                live = jnp.where(k < tile_count[0, 0, a], 1.0, 0.0).astype(F32)
                prod[q] = live * jnp.dot(v, turned[q * B:(q + 1) * B, :], preferred_element_type=F32)
        n = A * BPZ if t == 0 else BPZ
        copies = {}
        for r in order:
            for b in range(BPZ):
                for i, part in enumerate(parts(t, BPZ * (2 * z_peers[r] + 1 - core) + b)):
                    pr_send[t, r, i * BPZ + b] = part
            copies[r] = start(to_pair(pr_send.at[t, r, pl.ds(0, n)], pr_recv.at[t, r, pl.ds(0, n)],
                                      pr_ss.at[t, r], pr_rs.at[t, r]))
        for r in order:
            for b in range(BPZ):
                for i, part in enumerate(parts(t, BPZ * (2 * z_peers[r] + core) + b)):
                    keep[t, r, i * BPZ + b] = part
        return copies

    def spread(t, copies):
        n = A * BPZ if t == 0 else BPZ
        sends = last_sends if t == 0 else [(zs_send.at[t - 1], zs_recv.at[t - 1], t)]
        out = []
        for r in order:
            copies[r].wait_recv()
            for m in range(n):
                both = keep[t, r, m] + pr_recv[t, r, m]
                if r == 0:
                    keep[t, r, m] = both
                else:
                    i, at = last_place(m) if t == 0 else (0, m)
                    sends[i][0][r - 1, at] = both.astype(sends[i][0].dtype)
            if r:
                for send, recv, row in sends:
                    out.append(start(to_z(send.at[r - 1], recv.at[r - 1], zs_ss.at[row, r - 1], zs_rs.at[row, r - 1], r)))
        return out

    last_sends = [(zl_send, zl_recv, 0), (zh_send, zh_recv, H)]

    def last_place(m):
        a, b = m // BPZ, m % BPZ
        return b % 2, a * (BPZ // 2 if b % 2 else BPZ - BPZ // 2) + b // 2

    def summed(t, m):
        i, at = last_place(m) if t == 0 else (0, m)
        recv = last_sends[i][1] if t == 0 else zs_recv.at[t - 1]
        total = keep[t, 0, m]
        for r in range(1, Z):
            total = total + recv[r - 1, at].astype(F32)
        return total

    def crowding(t, now):
        own[t] = own[4] * jnp.log(1.0 + jnp.mean(now, axis=0, keepdims=True))

    def next_value(t, copies):
        reward = []
        for b in range(BPZ):
            cols = slice(b * B, (b + 1) * B)
            q0, q1 = own[5, :, cols], own[6, :, cols]
            reward.append(q0 * base_reward[0, :, cols] + q1 * base_reward[1, :, cols] - (q0 + q1) * own[t, :, cols])
        for copy in copies:
            copy.wait_recv()
        for b in range(BPZ):
            vbuf[t - 1][BPZ * s + b] = (reward[b] + DISCOUNT * summed(t, b)).astype(BF16)
        va[t - 1] = share_value(t - 1)

    for load in loads[7:]:
        load.wait()

    def turn(q, _):
        at = pl.ds(pl.multiple_of(q * B, B), B)
        turned[at, :] = tiles[at, :].T
        return _

    lax.fori_loop(0, A * K, turn, 0)
    relay(0, w0, w0_here, w0_here)
    mg_mine = margin.at[blocks_of(d)]
    mg_here = lambda r: margin.at[blocks_of(2 * z_back[r] + core)]
    mg = share(1, mg_mine, lambda r: mg_mine)
    pushed = push(0)
    crowding(0, rho)
    row_sums()
    raw, packed = owned(pushed)
    shared = share_density(0, raw, packed)
    relay(1, mg, mg_here, mg_here)

    def policy(g, _):
        for b in range(BPZ):
            c = g * BPZ + b
            pol[0, c] = jax.nn.sigmoid(margin[c])
            pol[1, c] = jax.nn.sigmoid(-margin[c])
        return _

    lax.fori_loop(0, D, policy, 0)
    now = take_density(0, raw, packed, shared)
    pushed = push(1)
    row_copies = [start(to_dst(row_send.at[dst_peers[r]], row_recv.at[r - 1], row_ss.at[r - 1], row_rs.at[r - 1], r))
                  for r in range(1, D)]
    crowding(1, now)
    pr = pull(3)
    raw, packed = owned(pushed)
    shared = share_density(1, raw, packed)
    now = take_density(1, raw, packed, shared)
    packed = own_mass(now, row_copies)
    col_send[...] = packed.astype(BF16)
    col_copies = [start(to_src(col_send, col_recv.at[r - 1], col_ss.at[r - 1], col_rs.at[r - 1], r)) for r in range(1, S)]
    pushed = push(2)
    for r in range(1, S):
        col_copies[r - 1].wait_recv()
        packed = packed + col_recv[r - 1].astype(F32)
    ms = send_mass(0, packed)
    crowding(2, now)
    zs = spread(3, pr)
    raw, _ = owned(pushed)
    ag3_send[...] = raw
    scale3 = take_mass(0, packed, ms)
    now = raw * scale3
    crowding(3, now)
    next_value(3, zs)
    shared = share(4, ag3_send, lambda r: ag3_recv.at[r])
    pr = pull(2)
    zs = spread(2, pr)
    relay(4, shared, lambda r: ag3_recv.at[r], lambda r: ag3_recv.at[Z + r])
    for b in range(BPZ):
        weigh(BPZ * d + b, raw[:, b * B:(b + 1) * B], scale3)
        for i in range(1, 2 * Z):
            weigh(BPZ * came_from(i) + b, ag3_recv[i, :, b * B:(b + 1) * B], scale3)
    next_value(2, zs)
    pushed = push(3)
    pr = pull(1)
    zs = spread(1, pr)
    raw, packed = owned(pushed)
    ms = send_mass(1, packed)
    next_value(1, zs)
    result[A + 1] = raw * take_mass(1, packed, ms)
    pr = pull(0)
    zs = spread(0, pr)
    for copy in zs:
        copy.wait_recv()
    for b in range(BPZ):
        cols = slice(b * B, (b + 1) * B)
        value = None
        for a in range(A):
            action_value = base_reward[a, :, cols] - own[0, :, cols] + DISCOUNT * summed(0, a * BPZ + b)
            result[a, :, cols] = logits[a, :, cols] + STEP_SIZE * action_value
            term = own[5 + a, :, cols] * action_value
            value = term if value is None else value + term
        result[A, :, cols] = value
    for copy in pending:
        copy.wait_send()


def deliver(A, result, new_logits, value_start, density_final):
    new_logits[...] = result[:A]
    value_start[...] = result[A]
    density_final[...] = result[A + 1]


def body(density0, logits, value_final, base_reward, crowd, tiles, tile_src, tile_dst, tile_count):
    S, D = lax.axis_size("src"), lax.axis_size("dst")
    PN, W = density0.shape
    A, K, B = tiles.shape[2], tiles.shape[3], tiles.shape[-1]
    BPZ = W // B
    SB, DB, Z = BPZ * D, BPZ * S, D // 2
    N = float(W * S * D)
    rows = -(-A * BPZ // 8) * 8
    dma = pltpu.SemaphoreType.DMA
    V = pltpu.VMEM
    args = (density0, logits, value_final, base_reward, crowd, tiles.reshape(A * K * B, B), tile_src, tile_dst, tile_count)
    places = (V, V, V, V, pltpu.SMEM, V, pltpu.SMEM, pltpu.SMEM, pltpu.SMEM)
    shared = dma((5, 2 * Z - 1))
    scratch = [place(x.shape, x.dtype) for place, x in zip(places, args)] + [
        dma((len(args),)), V((A * K * B, B), BF16),
        V((A, SB, PN, B), BF16), V((A, SB, PN, B), BF16), V((A, SB, PN, B), F32), V((SB, PN, B), F32),
        V((DB * PN, A * K * B), BF16), V((A * K * DB, PN, LANES), BF16), V((A * K, PN, B), F32), V((S, PN, W), F32),
        V((2, S, PN, W + LANES), BF16), V((2, S - 1, PN, W + LANES), BF16),
        V((H - 2, S, PN, W + LANES), F32), V((H - 2, S - 1, PN, W + LANES), F32),
        V((2, PN, W + LANES), BF16), V((2, 2 * Z, PN, W + LANES), BF16),
        V((PN, W), F32), V((2 * Z, PN, W), F32), V((2, PN, LANES), BF16), V((2, D - 1, PN, LANES), BF16),
        *[V((DB, PN, B), BF16)] * H,
        V((H, Z, A * BPZ, PN, B), F32), V((H, Z, A * BPZ, PN, B), F32),
        V((H - 1, Z - 1, BPZ, PN, B), BF16), V((H - 1, Z - 1, BPZ, PN, B), BF16),
        V((Z - 1, A * (BPZ - BPZ // 2), PN, B), F32), V((Z - 1, A * (BPZ - BPZ // 2), PN, B), F32),
        V((Z - 1, A * (BPZ // 2), PN, B), BF16), V((Z - 1, A * (BPZ // 2), PN, B), BF16),
        V((D, rows, B), F32), V((D - 1, rows, B), F32), V((PN, LANES), BF16), V((S - 1, PN, LANES), BF16),
        V((H, Z, A * BPZ, PN, B), F32), V((7, PN, W), F32),
        dma((H, S - 1)), dma((H, S - 1)), shared, shared, dma((2, D - 1)), dma((2, D - 1)),
        dma((H, S - 1)), dma((H, S - 1)), dma((H, Z)), dma((H, Z)), dma((H + 1, Z - 1)), dma((H + 1, Z - 1)),
        dma((D - 1,)), dma((D - 1,)), dma((S - 1,)), dma((S - 1,)),
    ]
    flops = 2 * H * 2 * A * K * PN * B * B
    out = pl.pallas_call(
        functools.partial(kernel, S, D, N, B, BPZ, A, K),
        out_shape=jax.ShapeDtypeStruct((A + 2, PN, W), F32),
        in_specs=[pl.BlockSpec(memory_space=pltpu.HBM)] * len(args),
        out_specs=pl.BlockSpec(memory_space=pltpu.VMEM),
        scratch_shapes=scratch,
        cost_estimate=pl.CostEstimate(flops=flops, bytes_accessed=tiles.size * 2, transcendentals=0),
        compiler_params=pltpu.CompilerParams(
            collective_id=0, has_side_effects=True, vmem_limit_bytes=62 * 1024 * 1024),
    )(*args)
    vmem = pl.BlockSpec(memory_space=pltpu.VMEM)
    return pl.pallas_call(
        functools.partial(deliver, A),
        out_shape=(jax.ShapeDtypeStruct((A, PN, W), F32),) + (jax.ShapeDtypeStruct((PN, W), F32),) * 2,
        in_specs=[vmem],
        out_specs=(vmem,) * 3,
        compiler_params=pltpu.CompilerParams(vmem_limit_bytes=62 * 1024 * 1024),
    )(out)


def solution(mesh):
    in_specs = (
        P(None, ("src", "dst")),
        P(None, None, ("src", "dst")),
        P(None, ("src", "dst")),
        P(None, None, ("src", "dst")),
        P(),
        P("src", "dst", None, None, None, None),
        P("src", "dst", None, None),
        P("src", "dst", None, None),
        P("src", "dst", None),
    )
    out_specs = (P(None, None, ("src", "dst")), P(None, ("src", "dst")), P(None, ("src", "dst")))
    return jax.shard_map(body, mesh=mesh, in_specs=in_specs, out_specs=out_specs, check_vma=False)
```

```python
import functools

import jax
import jax.numpy as jnp
from jax import lax
from jax.experimental import pallas as pl
from jax.experimental.pallas import tpu as pltpu
from jax.sharding import PartitionSpec as P

H = 4
LANES = 128
DISCOUNT = 0.9
STEP_SIZE = 1.0
MESH = pl.DeviceIdType.MESH
F32 = jnp.float32
BF16 = jnp.bfloat16


def kernel(
    S, D, N, B, BPZ, A, K,
    density0_h, logits_h, value_final_h, base_reward_h, crowd_h, tiles_h, tile_src_h, tile_dst_h, tile_count_h,
    result,
    density0, logits, value_final, base_reward, crowd, tiles, tile_src, tile_dst, tile_count, in_sem,
    turned, wbuf, w0buf, pol, margin, lhs, mask, prod, arr,
    rs_send, rs_recv, rz_send, rz_recv, ag_send, ag_recv, ag3_send, ag3_recv, ms_send, ms_recv,
    vb0, vb1, vb2, vb3, pr_send, pr_recv, zs_send, zs_recv, zl_send, zl_recv, zh_send, zh_recv, row_send, row_recv, col_send, col_recv, keep, own,
    rs_ss, rs_rs, sh_ss, sh_rs, ms_ss, ms_rs, va_ss, va_rs, pr_ss, pr_rs, zs_ss, zs_rs, row_ss, row_rs, col_ss, col_rs,
):
    vbuf = (vb0, vb1, vb2, vb3)
    s = lax.axis_index("src")
    d = lax.axis_index("dst")
    Z = D // 2
    z = d // 2
    core = d - 2 * z
    PN, W = density0.shape
    src_peers = [lax.rem(s + r, S) for r in range(S)]
    dst_peers = [lax.rem(d + r, D) for r in range(D)]
    z_peers = [lax.rem(z + r, Z) for r in range(Z)]
    z_back = [lax.rem(z + Z - r, Z) for r in range(Z)]

    def remote(src, dst, ss, rs, device):
        return pltpu.make_async_remote_copy(
            src_ref=src, dst_ref=dst, send_sem=ss, recv_sem=rs, device_id=device, device_id_type=MESH)

    def to_src(src, dst, ss, rs, r):
        return remote(src, dst, ss, rs, (src_peers[r], d))

    def to_dst(src, dst, ss, rs, r):
        return remote(src, dst, ss, rs, (s, dst_peers[r]))

    def to_z(src, dst, ss, rs, r):
        return remote(src, dst, ss, rs, (s, 2 * z_peers[r] + core))

    def to_pair(src, dst, ss, rs):
        return remote(src, dst, ss, rs, (s, 2 * z + 1 - core))

    loads = [pltpu.make_async_copy(h, v, in_sem.at[i]) for i, (h, v) in enumerate((
        (logits_h, logits), (density0_h, density0), (value_final_h, value_final), (tile_src_h, tile_src),
        (tile_dst_h, tile_dst), (tile_count_h, tile_count), (crowd_h, crowd), (base_reward_h, base_reward),
        (tiles_h, tiles)))]
    for load in loads:
        load.start()
    barrier = pltpu.get_barrier_semaphore()
    for r in range(1, S):
        pl.semaphore_signal(barrier, inc=1, device_id=(src_peers[r], d), device_id_type=MESH)
    for r in range(1, D):
        pl.semaphore_signal(barrier, inc=1, device_id=(s, dst_peers[r]), device_id_type=MESH)

    for load in loads[:3]:
        load.wait()
    gap = logits[0] - logits[1]
    p0, p1 = jax.nn.sigmoid(gap), jax.nn.sigmoid(-gap)
    rho = density0[...]
    vf = value_final[...].astype(BF16)
    for b in range(BPZ):
        cols = slice(b * B, (b + 1) * B)
        w0buf[0, BPZ * d + b] = (p0 * rho)[:, cols].astype(BF16)
        w0buf[1, BPZ * d + b] = (p1 * rho)[:, cols].astype(BF16)
        margin[BPZ * d + b] = gap[:, cols]
        vbuf[3][BPZ * s + b] = vf[:, cols]
    pl.semaphore_wait(barrier, S + D - 2)

    pending = []

    def start(copy):
        copy.start()
        pending.append(copy)
        return copy

    def share(i, own_ref, there):
        ss, rs = sh_ss.at[i], sh_rs.at[i]
        hops = [start(to_z(own_ref, there(r), ss.at[r - 1], rs.at[r - 1], r)) for r in range(1, Z)]
        return hops, start(to_pair(own_ref, there(Z), ss.at[Z - 1], rs.at[Z - 1]))

    def relay(i, shared, here, there):
        ss, rs = sh_ss.at[i], sh_rs.at[i]
        hops, pair = shared
        onward = []
        for r in range(1, Z):
            hops[r - 1].wait_recv()
            onward.append(start(to_pair(here(r), there(r), ss.at[Z - 1 + r], rs.at[Z - 1 + r])))
        pair.wait_recv()
        for copy in onward:
            copy.wait_recv()

    def blocks_of(j):
        return pl.ds(BPZ * j, BPZ)

    def came_from(i):
        return 2 * z_back[i % Z] + (core if i < Z else 1 - core)

    def share_value(t):
        at = vbuf[t].at[pl.ds(BPZ * s, BPZ)]
        return [start(to_src(at, at, va_ss.at[t, r - 1], va_rs.at[t, r - 1], r)) for r in range(1, S)]

    w0_mine = w0buf.at[:, blocks_of(d)]
    w0_here = lambda r: w0buf.at[:, blocks_of(2 * z_back[r] + core)]
    w0 = share(0, w0_mine, lambda r: w0_mine)
    va = {3: share_value(3)}

    for load in loads[3:7]:
        load.wait()
    for a in range(A):
        for k in range(K):
            live = jnp.where(k < tile_count[0, 0, a], 1.0, 0.0).astype(F32)
            for c in range(BPZ * S):
                hit = jnp.where(tile_dst[0, 0, a, k] == c, live, 0.0)
                mask[(a * K + k) * BPZ * S + c] = jnp.full((PN, LANES), hit, F32).astype(BF16)
    row = lax.broadcasted_iota(jnp.int32, (PN, W), 0)
    crowd_col = jnp.zeros((PN, W), F32)
    for p in range(PN):
        crowd_col = jnp.where(row == p, crowd[p], crowd_col)
    own[4] = crowd_col
    own[5] = p0
    own[6] = p1
    lane = lax.broadcasted_iota(jnp.int32, (PN, LANES), 1)
    DB = BPZ * S

    def pack(terms):
        mass = jnp.broadcast_to(jnp.sum(terms, axis=1, keepdims=True), (PN, LANES))
        hi = mass.astype(BF16).astype(F32)
        mid = (mass - hi).astype(BF16).astype(F32)
        low = (mass - hi - mid).astype(BF16).astype(F32)
        return jnp.where(lane == 3 * s, hi, jnp.where(lane == 3 * s + 1, mid, jnp.where(lane == 3 * s + 2, low, 0.0)))

    def push(t):
        for a in range(A):
            for k in range(K):
                w = (w0buf if t == 0 else wbuf)[a, tile_src[0, 0, a, k]]
                q = a * K + k
                for c in range(DB):
                    m = mask[q * DB + c]
                    lhs[c * PN:(c + 1) * PN, q * B:(q + 1) * B] = w * jnp.concatenate([m] * (B // LANES), axis=1)
        arrived = jnp.dot(lhs[...], tiles[...], preferred_element_type=F32)
        send, recv = (rs_send.at[t], rs_recv.at[t]) if t < 2 else (rz_send.at[t - 2], rz_recv.at[t - 2])
        for c in range(DB):
            part = arrived[c * PN:(c + 1) * PN]
            at = slice((c % BPZ) * B, (c % BPZ + 1) * B)
            arr[c // BPZ, :, at] = part
            send[c // BPZ, :, at] = part.astype(send.dtype)
        if t == 2:
            packed, width = None, W
        else:
            total = arrived[0:PN]
            for c in range(1, DB):
                total = total + arrived[c * PN:(c + 1) * PN]
            packed, width = pack(total), W + LANES
            for c in range(S):
                send[c, :, W:W + LANES] = packed.astype(send.dtype)
        cut = (slice(None), pl.ds(0, width))
        copies = [start(to_src(send.at[(src_peers[r],) + cut], recv.at[(r - 1,) + cut], rs_ss.at[t, r - 1], rs_rs.at[t, r - 1], r))
                  for r in range(1, S)]
        return copies, recv, packed

    def owned(pushed):
        copies, recv, packed = pushed
        raw = arr[s]
        for r in range(1, S):
            copies[r - 1].wait_recv()
            raw = raw + recv[r - 1, :, :W].astype(F32)
            if packed is not None:
                packed = packed + recv[r - 1, :, W:W + LANES].astype(F32)
        return raw, packed

    def scale_of(packed):
        mass = jnp.sum(packed, axis=1, keepdims=True)
        return N / mass

    def weigh(block, raw, scale):
        now = raw * scale
        wbuf[0, block] = (pol[0, block] * now).astype(BF16)
        wbuf[1, block] = (pol[1, block] * now).astype(BF16)

    def share_density(t, raw, packed):
        ag_send[t, :, :W] = raw.astype(BF16)
        ag_send[t, :, W:W + LANES] = packed.astype(BF16)
        return share(2 + t, ag_send.at[t], lambda r: ag_recv.at[t, r])

    def take_density(t, raw, packed, shared):
        slot = lambda r: ag_recv.at[t, r]
        relay(2 + t, shared, slot, lambda r: ag_recv.at[t, Z + r])
        for i in range(1, 2 * Z):
            packed = packed + ag_recv[t, i, :, W:W + LANES].astype(F32)
        scale = scale_of(packed)
        for b in range(BPZ):
            weigh(BPZ * d + b, raw[:, b * B:(b + 1) * B], scale)
        for i in range(1, 2 * Z):
            for b in range(BPZ):
                weigh(BPZ * came_from(i) + b, ag_recv[t, i, :, b * B:(b + 1) * B].astype(F32), scale)
        return raw * scale

    def send_mass(i, packed):
        ms_send[i] = packed.astype(BF16)
        return [start(to_dst(ms_send.at[i], ms_recv.at[i, r - 1], ms_ss.at[i, r - 1], ms_rs.at[i, r - 1], r))
                for r in range(1, D)]

    def take_mass(i, packed, copies):
        for r in range(1, D):
            copies[r - 1].wait_recv()
            packed = packed + ms_recv[i, r - 1].astype(F32)
        return scale_of(packed)

    def collect(a, block):
        out = None
        for k in range(K):
            term = jnp.where(tile_src[0, 0, a, k] == block, 1.0, 0.0).astype(F32) * prod[a * K + k]
            out = term if out is None else out + term
        return out

    def parts(t, block):
        out = [collect(a, block) for a in range(A)]
        return out if t == 0 else [pol[0, block] * out[0] + pol[1, block] * out[1]]

    order = list(range(1, Z)) + [0]

    def row_sums():
        ones = jnp.ones((PN, B), BF16)
        for a in range(A):
            for k in range(K):
                q = a * K + k
                live = jnp.where(k < tile_count[0, 0, a], 1.0, 0.0).astype(F32)
                prod[q] = live * jnp.dot(ones, turned[q * B:(q + 1) * B, :], preferred_element_type=F32)
        rows = row_send.shape[1]
        which = lax.broadcasted_iota(jnp.int32, (rows, B), 0)

        def one(j, _):
            out = jnp.zeros((rows, B), F32)
            for m in range(A * BPZ):
                part = collect(m // BPZ, BPZ * j + m % BPZ)[0:1]
                out = jnp.where(which == m, jnp.broadcast_to(part, (rows, B)), out)
            row_send[j] = out
            return _

        lax.fori_loop(0, D, one, 0)

    def own_mass(now, copies):
        total = row_send[d]
        for r in range(1, D):
            copies[r - 1].wait_recv()
            total = total + row_recv[r - 1]
        terms = jnp.zeros((PN, B), F32)
        for m in range(A * BPZ):
            cols = slice((m % BPZ) * B, (m % BPZ + 1) * B)
            w = (own[5 + m // BPZ, :, cols] * now[:, cols]).astype(BF16).astype(F32)
            terms = terms + w * total[m:m + 1]
        return pack(terms)

    def pull(t):
        for copy in va[t]:
            copy.wait_recv()
        for a in range(A):
            for k in range(K):
                q = a * K + k
                v = vbuf[t][tile_dst[0, 0, a, k]]
                live = jnp.where(k < tile_count[0, 0, a], 1.0, 0.0).astype(F32)
                prod[q] = live * jnp.dot(v, turned[q * B:(q + 1) * B, :], preferred_element_type=F32)
        n = A * BPZ if t == 0 else BPZ
        copies = {}
        for r in order:
            for b in range(BPZ):
                for i, part in enumerate(parts(t, BPZ * (2 * z_peers[r] + 1 - core) + b)):
                    pr_send[t, r, i * BPZ + b] = part
            copies[r] = start(to_pair(pr_send.at[t, r, pl.ds(0, n)], pr_recv.at[t, r, pl.ds(0, n)],
                                      pr_ss.at[t, r], pr_rs.at[t, r]))
        for r in order:
            for b in range(BPZ):
                for i, part in enumerate(parts(t, BPZ * (2 * z_peers[r] + core) + b)):
                    keep[t, r, i * BPZ + b] = part
        return copies

    def spread(t, copies):
        n = A * BPZ if t == 0 else BPZ
        sends = last_sends if t == 0 else [(zs_send.at[t - 1], zs_recv.at[t - 1], t)]
        out = []
        for r in order:
            copies[r].wait_recv()
            for m in range(n):
                both = keep[t, r, m] + pr_recv[t, r, m]
                if r == 0:
                    keep[t, r, m] = both
                else:
                    i, at = last_place(m) if t == 0 else (0, m)
                    sends[i][0][r - 1, at] = both.astype(sends[i][0].dtype)
            if r:
                for send, recv, row in sends:
                    out.append(start(to_z(send.at[r - 1], recv.at[r - 1], zs_ss.at[row, r - 1], zs_rs.at[row, r - 1], r)))
        return out

    last_sends = [(zl_send, zl_recv, 0), (zh_send, zh_recv, H)]

    def last_place(m):
        a, b = m // BPZ, m % BPZ
        return b % 2, a * (BPZ // 2 if b % 2 else BPZ - BPZ // 2) + b // 2

    def summed(t, m):
        i, at = last_place(m) if t == 0 else (0, m)
        recv = last_sends[i][1] if t == 0 else zs_recv.at[t - 1]
        total = keep[t, 0, m]
        for r in range(1, Z):
            total = total + recv[r - 1, at].astype(F32)
        return total

    def crowding(t, now):
        own[t] = own[4] * jnp.log(1.0 + jnp.mean(now, axis=0, keepdims=True))

    def next_value(t, copies):
        reward = []
        for b in range(BPZ):
            cols = slice(b * B, (b + 1) * B)
            q0, q1 = own[5, :, cols], own[6, :, cols]
            reward.append(q0 * base_reward[0, :, cols] + q1 * base_reward[1, :, cols] - (q0 + q1) * own[t, :, cols])
        for copy in copies:
            copy.wait_recv()
        for b in range(BPZ):
            vbuf[t - 1][BPZ * s + b] = (reward[b] + DISCOUNT * summed(t, b)).astype(BF16)
        va[t - 1] = share_value(t - 1)

    for load in loads[7:]:
        load.wait()

    def turn(q, _):
        at = pl.ds(pl.multiple_of(q * B, B), B)
        turned[at, :] = tiles[at, :].T
        return _

    lax.fori_loop(0, A * K, turn, 0)
    relay(0, w0, w0_here, w0_here)
    mg_mine = margin.at[blocks_of(d)]
    mg_here = lambda r: margin.at[blocks_of(2 * z_back[r] + core)]
    mg = share(1, mg_mine, lambda r: mg_mine)
    pushed = push(0)
    crowding(0, rho)
    row_sums()
    raw, packed = owned(pushed)
    shared = share_density(0, raw, packed)
    relay(1, mg, mg_here, mg_here)

    def policy(g, _):
        for b in range(BPZ):
            c = g * BPZ + b
            pol[0, c] = jax.nn.sigmoid(margin[c])
            pol[1, c] = jax.nn.sigmoid(-margin[c])
        return _

    lax.fori_loop(0, D, policy, 0)
    now = take_density(0, raw, packed, shared)
    pushed = push(1)
    row_copies = [start(to_dst(row_send.at[dst_peers[r]], row_recv.at[r - 1], row_ss.at[r - 1], row_rs.at[r - 1], r))
                  for r in range(1, D)]
    crowding(1, now)
    pr = pull(3)
    raw, packed = owned(pushed)
    shared = share_density(1, raw, packed)
    now = take_density(1, raw, packed, shared)
    packed = own_mass(now, row_copies)
    col_send[...] = packed.astype(BF16)
    col_copies = [start(to_src(col_send, col_recv.at[r - 1], col_ss.at[r - 1], col_rs.at[r - 1], r)) for r in range(1, S)]
    pushed = push(2)
    for r in range(1, S):
        col_copies[r - 1].wait_recv()
        packed = packed + col_recv[r - 1].astype(F32)
    ms = send_mass(0, packed)
    crowding(2, now)
    zs = spread(3, pr)
    raw, _ = owned(pushed)
    ag3_send[...] = raw
    scale3 = take_mass(0, packed, ms)
    now = raw * scale3
    crowding(3, now)
    next_value(3, zs)
    shared = share(4, ag3_send, lambda r: ag3_recv.at[r])
    pr = pull(2)
    zs = spread(2, pr)
    relay(4, shared, lambda r: ag3_recv.at[r], lambda r: ag3_recv.at[Z + r])
    for b in range(BPZ):
        weigh(BPZ * d + b, raw[:, b * B:(b + 1) * B], scale3)
        for i in range(1, 2 * Z):
            weigh(BPZ * came_from(i) + b, ag3_recv[i, :, b * B:(b + 1) * B], scale3)
    next_value(2, zs)
    pushed = push(3)
    pr = pull(1)
    zs = spread(1, pr)
    raw, packed = owned(pushed)
    ms = send_mass(1, packed)
    next_value(1, zs)
    result[A + 1] = raw * take_mass(1, packed, ms)
    pr = pull(0)
    zs = spread(0, pr)
    for copy in zs:
        copy.wait_recv()
    for b in range(BPZ):
        cols = slice(b * B, (b + 1) * B)
        value = None
        for a in range(A):
            action_value = base_reward[a, :, cols] - own[0, :, cols] + DISCOUNT * summed(0, a * BPZ + b)
            result[a, :, cols] = logits[a, :, cols] + STEP_SIZE * action_value
            term = own[5 + a, :, cols] * action_value
            value = term if value is None else value + term
        result[A, :, cols] = value
    for copy in pending:
        copy.wait_send()


def deliver(A, result, new_logits, value_start, density_final):
    new_logits[...] = result[:A]
    value_start[...] = result[A]
    density_final[...] = result[A + 1]


def body(density0, logits, value_final, base_reward, crowd, tiles, tile_src, tile_dst, tile_count):
    S, D = lax.axis_size("src"), lax.axis_size("dst")
    PN, W = density0.shape
    A, K, B = tiles.shape[2], tiles.shape[3], tiles.shape[-1]
    BPZ = W // B
    SB, DB, Z = BPZ * D, BPZ * S, D // 2
    N = float(W * S * D)
    rows = -(-A * BPZ // 8) * 8
    dma = pltpu.SemaphoreType.DMA
    V = pltpu.VMEM
    args = (density0, logits, value_final, base_reward, crowd, tiles.reshape(A * K * B, B), tile_src, tile_dst, tile_count)
    places = (V, V, V, V, pltpu.SMEM, V, pltpu.SMEM, pltpu.SMEM, pltpu.SMEM)
    shared = dma((5, 2 * Z - 1))
    scratch = [place(x.shape, x.dtype) for place, x in zip(places, args)] + [
        dma((len(args),)), V((A * K * B, B), BF16),
        V((A, SB, PN, B), BF16), V((A, SB, PN, B), BF16), V((A, SB, PN, B), F32), V((SB, PN, B), F32),
        V((DB * PN, A * K * B), BF16), V((A * K * DB, PN, LANES), BF16), V((A * K, PN, B), F32), V((S, PN, W), F32),
        V((2, S, PN, W + LANES), BF16), V((2, S - 1, PN, W + LANES), BF16),
        V((H - 2, S, PN, W + LANES), F32), V((H - 2, S - 1, PN, W + LANES), F32),
        V((2, PN, W + LANES), BF16), V((2, 2 * Z, PN, W + LANES), BF16),
        V((PN, W), F32), V((2 * Z, PN, W), F32), V((2, PN, LANES), BF16), V((2, D - 1, PN, LANES), BF16),
        *[V((DB, PN, B), BF16)] * H,
        V((H, Z, A * BPZ, PN, B), F32), V((H, Z, A * BPZ, PN, B), F32),
        V((H - 1, Z - 1, BPZ, PN, B), BF16), V((H - 1, Z - 1, BPZ, PN, B), BF16),
        V((Z - 1, A * (BPZ - BPZ // 2), PN, B), F32), V((Z - 1, A * (BPZ - BPZ // 2), PN, B), F32),
        V((Z - 1, A * (BPZ // 2), PN, B), BF16), V((Z - 1, A * (BPZ // 2), PN, B), BF16),
        V((D, rows, B), F32), V((D - 1, rows, B), F32), V((PN, LANES), BF16), V((S - 1, PN, LANES), BF16),
        V((H, Z, A * BPZ, PN, B), F32), V((7, PN, W), F32),
        dma((H, S - 1)), dma((H, S - 1)), shared, shared, dma((2, D - 1)), dma((2, D - 1)),
        dma((H, S - 1)), dma((H, S - 1)), dma((H, Z)), dma((H, Z)), dma((H + 1, Z - 1)), dma((H + 1, Z - 1)),
        dma((D - 1,)), dma((D - 1,)), dma((S - 1,)), dma((S - 1,)),
    ]
    flops = 2 * H * 2 * A * K * PN * B * B
    out = pl.pallas_call(
        functools.partial(kernel, S, D, N, B, BPZ, A, K),
        out_shape=jax.ShapeDtypeStruct((A + 2, PN, W), F32),
        in_specs=[pl.BlockSpec(memory_space=pltpu.HBM)] * len(args),
        out_specs=pl.BlockSpec(memory_space=pltpu.VMEM),
        scratch_shapes=scratch,
        cost_estimate=pl.CostEstimate(flops=flops, bytes_accessed=tiles.size * 2, transcendentals=0),
        compiler_params=pltpu.CompilerParams(
            collective_id=0, has_side_effects=True, vmem_limit_bytes=62 * 1024 * 1024),
    )(*args)
    vmem = pl.BlockSpec(memory_space=pltpu.VMEM)
    return pl.pallas_call(
        functools.partial(deliver, A),
        out_shape=(jax.ShapeDtypeStruct((A, PN, W), F32),) + (jax.ShapeDtypeStruct((PN, W), F32),) * 2,
        in_specs=[vmem],
        out_specs=(vmem,) * 3,
        compiler_params=pltpu.CompilerParams(vmem_limit_bytes=62 * 1024 * 1024),
    )(out)


def solution(mesh):
    in_specs = (
        P(None, ("src", "dst")),
        P(None, None, ("src", "dst")),
        P(None, ("src", "dst")),
        P(None, None, ("src", "dst")),
        P(),
        P("src", "dst", None, None, None, None),
        P("src", "dst", None, None),
        P("src", "dst", None, None),
        P("src", "dst", None),
    )
    out_specs = (P(None, None, ("src", "dst")), P(None, ("src", "dst")), P(None, ("src", "dst")))
    return jax.shard_map(body, mesh=mesh, in_specs=in_specs, out_specs=out_specs, check_vma=False)
```
